32 devices in a mesh: lat: 4 (over z), chan: 2 (over core), obs: 4 (over y, x).
Axes of the slice: x: 2, y: 2, z: 4, core: 2. Of those that a mesh axis runs over, the one named last changes fastest.
Arguments:
- next_grad: bfloat16 [32, 1024, 256], P(('lat', 'obs'), None, 'chan'), may hold values from -6 to 6
- pre_act: bfloat16 [32, 1024, 256], P(('lat', 'obs'), None, 'chan'), may hold values from -6 to 6
- legendre: bfloat16 [512, 512, 32], P(('lat', 'obs')), may hold values from -1 to 1, as said below
- order_slots: int32 [512], replicated, may hold values from 0 to 511, as said below
- quad_weights: float32 [32], replicated, may hold values from 0.5 to 1.5
- spectral_gain: float32 [2, 512, 256], P(None, None, 'chan'), may hold values from -5 to 5
- saved_coeffs: bfloat16 [512, 2, 512, 256], P(('lat', 'obs'), None, None, 'chan'), may hold values from -0.029907227 to 0.029907227
- obs_value: bfloat16 [16, 16, 16], P(('lat', 'obs')), may hold values from -16 to 16
- obs_lat_frac: bfloat16 [16, 16, 16], P(('lat', 'obs')), may hold values from 0 to 1
- obs_lon_frac: bfloat16 [16, 16, 16], P(('lat', 'obs')), may hold values from 0 to 1
- obs_corner: int32 [16, 16, 16], P(('lat', 'obs')), may hold values from 0 to 1023
- obs_channel: int32 [16, 16, 16], P(('lat', 'obs')), may hold values from 0 to 255
- slot_counts: int32 [16, 16], P(('lat', 'obs')), may hold values from 0 to 16, as said below
Outputs:
- grid_grad: bfloat16 [32, 1024, 256], P(('lat', 'obs'), None, 'chan')
- gain_grad: float32 [2, 512, 256], P(None, None, 'chan')
The draws below stay inside these ranges and needn't reach their ends.
Inputs may be any that keep to these rules, and one draw needn't show every extreme that they name: `order_slots`: each order from 0 to 511 stands at exactly one slot. `legendre`: entry [s, l, lat] is zero wherever l < order_slots[s]. `slot_counts`: at most 16; in every draw some tile receives 16 live slots from every source shard; slots at or beyond the count carry no observation.
All inputs are finite; a program needn't handle non-finite values.
Results may differ from the reference program's by a relative error of at most 0.0055.
Values may be sent and summed in bfloat16 or wider, within the bound.
A program may use at most 128 MiB of HBM per device.

```python
import math
import jax
import jax.numpy as jnp
from jax import lax

C = 256
NLON = 1024
L = 512
LAT_DEV = 2
CAP = 16
M = 512
NLAT = 32
SOURCES = 16
DESTS = 16


def shared_orders(key):
    return jax.random.permutation(key, M).astype(jnp.int32)


def draw_order_slots(key, part):
    return shared_orders(key)


def draw_legendre(key, part):
    orders = shared_orders(key)
    key = jax.random.fold_in(key, 3)
    scale = NLAT ** (-0.5)
    values = jnp.clip(jax.random.normal(key, (M, L, NLAT), jnp.float32) * scale, -1.0, 1.0)
    degrees = lax.iota(jnp.int32, L)
    keep = degrees[None, :, None] >= orders[:, None, None]
    return jnp.where(keep, values, 0.0).astype(jnp.bfloat16)


def draw_slot_counts(key, part):
    key = jax.random.fold_in(key, 5)
    base_key, heavy_key, chosen_key = jax.random.split(key, 3)
    base = jax.random.randint(base_key, (SOURCES, DESTS), 0, CAP + 1)
    heavy = jax.random.randint(heavy_key, (DESTS,), 0, 8) == 0
    chosen = jax.random.randint(chosen_key, (), 0, DESTS)
    heavy = heavy | (lax.iota(jnp.int32, DESTS) == chosen)
    return jnp.where(heavy[None, :], CAP, base).astype(jnp.int32)


def touch_ends(result, rng, smallest, largest):
    extent = result.shape
    index_at = [jax.random.randint(jax.random.fold_in(rng, axis), (), 0, extent[axis]) for axis in range(len(extent))]
    result = result.at[tuple(index_at)].set(smallest)
    longest = extent.index(max(extent))
    index_at[longest] = (index_at[longest] + 1) % extent[longest]
    return result.at[tuple(index_at)].set(largest)


def level_of(stream_key, extent, pieces, least, top_value):
    loudness, own = 1.0, jax.random.fold_in(stream_key, 6)
    for position, blocks in pieces:
        heights = jnp.exp(jax.random.uniform(jax.random.fold_in(own, position), (blocks,), jnp.float32, least / len(pieces), top_value / len(pieces)))
        loudness = loudness * jnp.repeat(heights, extent[position] // blocks).reshape([-1 if axis == position else 1 for axis in range(len(extent))])
    return loudness


def normal_values(rng, extent, spread, reach, cuts=(), kind=jnp.bfloat16):
    values = spread * jax.random.normal(rng, extent, jnp.float32)
    if cuts:
        values = values * level_of(rng, extent, cuts, -0.22, 0.18)
    return jnp.clip(values, -reach, reach).astype(kind)


def setup_inputs(seed: int = 0) -> dict:
    key_list = jax.random.split(jax.random.key(seed), 14)
    return {
        "next_grad": normal_values(key_list[0], (NLAT, NLON, C), 1.0, 6.0, ((0, 16), (2, 2))),
        "pre_act": normal_values(key_list[1], (NLAT, NLON, C), 1.0, 6.0, ((0, 16), (2, 2))),
        "legendre": draw_legendre(jax.random.fold_in(key_list[13], 71), 0),
        "order_slots": draw_order_slots(jax.random.fold_in(key_list[13], 71), 0),
        "quad_weights": jnp.clip(jax.random.uniform(key_list[4], (NLAT,), jnp.float32, 0.5, 1.5), 0.5, 1.5),
        "spectral_gain": normal_values(key_list[5], (2, L, C), 1.0, 5.0, ((2, 2),), jnp.float32),
        "saved_coeffs": normal_values(key_list[6], (M, 2, L, C), 0.005, 0.029907227, ((0, 16), (3, 2))),
        "obs_value": normal_values(key_list[7], (SOURCES, CAP, DESTS), 4.0, 16.0, ((0, 16),)),
        "obs_lat_frac": jnp.clip(1.0 * jax.random.uniform(key_list[8], (SOURCES, CAP, DESTS), jnp.float32) ** level_of(key_list[8], (SOURCES, CAP, DESTS), ((0, 16),), -0.2, 0.2), 0.0, 1.0).astype(jnp.bfloat16),
        "obs_lon_frac": jnp.clip(1.0 * jax.random.uniform(key_list[9], (SOURCES, CAP, DESTS), jnp.float32) ** level_of(key_list[9], (SOURCES, CAP, DESTS), ((0, 16),), -0.2, 0.2), 0.0, 1.0).astype(jnp.bfloat16),
        "obs_corner": touch_ends(jax.random.randint(key_list[10], (SOURCES, CAP, DESTS), 0, (LAT_DEV - 1) * NLON), jax.random.fold_in(key_list[10], 1), 0, ((LAT_DEV - 1) * NLON) - 1).astype(jnp.int32),
        "obs_channel": touch_ends(jax.random.randint(key_list[11], (SOURCES, CAP, DESTS), 0, C), jax.random.fold_in(key_list[11], 1), 0, C - 1).astype(jnp.int32),
        "slot_counts": draw_slot_counts(jax.random.fold_in(key_list[13], 71), 0),
    }


def gelu_slope(pre_act):
    values = pre_act.astype(jnp.float32)
    normal_cdf = 0.5 * (1.0 + jax.scipy.special.erf(values * 0.7071067811865476))
    density = jnp.exp(-0.5 * values * values) * 0.3989422804014327
    return normal_cdf + values * density


def zonal_tables(orders, longitudes, lon_count, cos_weight, sin_weight):
    phase = (orders[:, None] * longitudes[None, :]) % lon_count
    angle = phase.astype(jnp.float32) * (2.0 * math.pi / lon_count)
    return (cos_weight * jnp.cos(angle)).astype(jnp.bfloat16), (sin_weight * jnp.sin(angle)).astype(jnp.bfloat16)


def observe(obs_value, obs_lat_frac, obs_lon_frac, obs_corner, obs_channel, slot_counts):
    alive_slots = lax.iota(jnp.int32, CAP)[None, :, None] < slot_counts[:, None, :]
    amounts = jnp.where(alive_slots, obs_value, jnp.zeros((), jnp.bfloat16)).astype(jnp.float32)
    lat_step = obs_lat_frac.astype(jnp.float32)
    lon_step = obs_lon_frac.astype(jnp.float32)
    top = obs_corner // NLON
    left = obs_corner % NLON
    right = (left + 1) % NLON
    tile_rows = lax.iota(jnp.int32, DESTS)[None, None, :] * LAT_DEV + top
    lower = tile_rows * NLON
    upper = lower + NLON
    weights = ((1.0 - lat_step) * (1.0 - lon_step), (1.0 - lat_step) * lon_step, lat_step * (1.0 - lon_step), lat_step * lon_step)
    places = (lower + left, lower + right, upper + left, upper + right)
    field = jnp.zeros((NLAT * NLON * C,), jnp.float32)
    for weight, place in zip(weights, places):
        rounded = lax.optimization_barrier(weight.astype(jnp.bfloat16)).astype(jnp.float32)
        flat_index = (place * C + obs_channel).reshape(-1).astype(jnp.int32)
        field = field.at[flat_index].add((rounded * amounts).reshape(-1))
    return field.reshape(NLAT, NLON, C)


def reference(next_grad, pre_act, legendre, order_slots, quad_weights, spectral_gain, saved_coeffs, obs_value, obs_lat_frac, obs_lon_frac, obs_corner, obs_channel, slot_counts):
    out_grad = next_grad.astype(jnp.float32) + observe(obs_value, obs_lat_frac, obs_lon_frac, obs_corner, obs_channel, slot_counts)
    pre_grad = (out_grad * gelu_slope(pre_act)).astype(jnp.bfloat16)
    orders = lax.iota(jnp.int32, M)
    longitudes = lax.iota(jnp.int32, NLON)
    factor = jnp.where(orders == 0, 1.0, 2.0).astype(jnp.float32)[:, None]
    syn_cos, syn_sin = zonal_tables(orders, longitudes, NLON, factor, -factor)
    pre_wide = pre_grad.astype(jnp.float32)
    real_part = jnp.einsum("mn,knc->mkc", syn_cos.astype(jnp.float32), pre_wide)
    imag_part = jnp.einsum("mn,knc->mkc", syn_sin.astype(jnp.float32), pre_wide)
    fourier_grad = jnp.stack([real_part, imag_part], axis=1).astype(jnp.bfloat16)
    gain_real = spectral_gain[0].astype(jnp.float32)
    gain_imag = spectral_gain[1].astype(jnp.float32)

    def per_slot(summed, slot):
        table = lax.dynamic_index_in_dim(legendre, slot, 0, keepdims=False).astype(jnp.float32)
        order = lax.dynamic_index_in_dim(order_slots, slot, 0, keepdims=False)
        fourier = lax.dynamic_index_in_dim(fourier_grad, order, 0, keepdims=False).astype(jnp.float32)
        up_grad = jnp.einsum("lk,rkc->rlc", table, fourier)
        saved = lax.dynamic_index_in_dim(saved_coeffs, slot, 0, keepdims=False).astype(jnp.float32)
        summed = summed + jnp.stack([up_grad[0] * saved[0] + up_grad[1] * saved[1], up_grad[1] * saved[0] - up_grad[0] * saved[1]])
        coeff_grad = jnp.stack([gain_real * up_grad[0] + gain_imag * up_grad[1], gain_real * up_grad[1] - gain_imag * up_grad[0]])
        coeff_wide = lax.optimization_barrier(coeff_grad.astype(jnp.bfloat16)).astype(jnp.float32)
        lat_grad = (jnp.einsum("lk,rlc->rkc", table, coeff_wide) * quad_weights[None, :, None]).astype(jnp.bfloat16)
        return summed, lat_grad

    gain_grad, lat_grad = lax.scan(per_slot, jnp.zeros((2, L, C), jnp.float32), lax.iota(jnp.int32, M))
    scale = jnp.full((M, 1), 1.0 / NLON, jnp.float32)
    ana_cos, ana_sin = zonal_tables(order_slots, longitudes, NLON, scale, -scale)
    spectral_grad = jnp.einsum("sn,skc->knc", ana_cos.astype(jnp.float32), lat_grad[:, 0].astype(jnp.float32))
    spectral_grad = spectral_grad + jnp.einsum("sn,skc->knc", ana_sin.astype(jnp.float32), lat_grad[:, 1].astype(jnp.float32))
    grid_grad = (out_grad + spectral_grad).astype(jnp.bfloat16)
    return grid_grad, gain_grad
```

```python
import functools
import math

import jax
import jax.numpy as jnp
import numpy as np
from jax import lax
from jax.experimental import pallas as pl
from jax.experimental.pallas import tpu as pltpu
from jax.sharding import PartitionSpec as P


def gelu_slope(pre_act):
    values = pre_act.astype(jnp.float32)
    normal_cdf = 0.5 * (1.0 + jax.scipy.special.erf(values * 0.7071067811865476))
    density = jnp.exp(-0.5 * values * values) * 0.3989422804014327
    return normal_cdf + values * density


def zonal_tables(orders, longitudes, lon_count, cos_weight, sin_weight):
    phase = orders[:, None] * longitudes[None, :] % lon_count
    angle = phase.astype(jnp.float32) * (2.0 * math.pi / lon_count)
    return (
        (cos_weight * jnp.cos(angle)).astype(jnp.bfloat16),
        (sin_weight * jnp.sin(angle)).astype(jnp.bfloat16),
    )


def adjoint_tiles(
    amounts, lat_frac, lon_frac, corners, channels, lat_dev, lon_count, chan_base, width
):
    received = amounts.size
    amounts = amounts.reshape(received)
    lat_frac = lat_frac.reshape(received)
    lon_frac = lon_frac.reshape(received)
    corners = corners.reshape(received)
    channels = channels.reshape(received)
    block_rows = min(512, received)
    cell_ids = lax.iota(jnp.int32, lat_dev * lon_count)
    chan_ids = chan_base + lax.iota(jnp.int32, width)
    nothing = jnp.zeros((), jnp.bfloat16)

    def add_block(counter, summed):
        offset = counter * block_rows
        lat_step = lax.dynamic_slice_in_dim(lat_frac, offset, block_rows).astype(jnp.float32)
        lon_step = lax.dynamic_slice_in_dim(lon_frac, offset, block_rows).astype(jnp.float32)
        corner_ids = lax.dynamic_slice_in_dim(corners, offset, block_rows)
        chan_rows = lax.dynamic_slice_in_dim(channels, offset, block_rows)
        amount_rows = lax.dynamic_slice_in_dim(amounts, offset, block_rows)
        top = corner_ids // lon_count
        left = corner_ids % lon_count
        right = (left + 1) % lon_count
        lower = top * lon_count
        upper = lower + lon_count
        weights = (
            (1.0 - lat_step) * (1.0 - lon_step),
            (1.0 - lat_step) * lon_step,
            lat_step * (1.0 - lon_step),
            lat_step * lon_step,
        )
        places = (lower + left, lower + right, upper + left, upper + right)
        stencil = jnp.zeros((block_rows, lat_dev * lon_count), jnp.bfloat16)
        for weight, place in zip(weights, places):
            stencil = stencil + jnp.where(
                cell_ids[None, :] == place[:, None], weight.astype(jnp.bfloat16)[:, None], nothing
            )
        sources = jnp.where(chan_rows[:, None] == chan_ids[None, :], amount_rows[:, None], nothing)
        return summed + lax.dot_general(
            stencil, sources, (((0,), (0,)), ((), ())), preferred_element_type=jnp.float32
        )

    start_sum = jnp.zeros((lat_dev * lon_count, width), jnp.float32)
    summed = lax.fori_loop(0, received // block_rows, add_block, start_sum)
    return summed.reshape(lat_dev, lon_count, width)


def plain_path(
    next_grad,
    pre_act,
    legendre,
    order_slots,
    quad_weights,
    spectral_gain,
    saved_coeffs,
    obs_value,
    obs_lat_frac,
    obs_lon_frac,
    obs_corner,
    obs_channel,
    slot_counts,
):
    lat_dev, lon_count, width = next_grad.shape
    lat_size = lax.axis_size("lat")
    obs_size = lax.axis_size("obs")
    slot_dev, degrees, lat_count = legendre.shape
    total_orders = order_slots.shape[0]
    capacity = obs_value.shape[1]
    alive_slots = lax.iota(jnp.int32, capacity)[:, None] < slot_counts[0][None, :]
    masked = jnp.where(alive_slots, obs_value[0], jnp.zeros((), jnp.bfloat16)).reshape(
        capacity, lat_size, obs_size
    )
    lat_frac = obs_lat_frac[0].reshape(capacity, lat_size, obs_size)
    lon_frac = obs_lon_frac[0].reshape(capacity, lat_size, obs_size)
    corners = obs_corner[0].reshape(capacity, lat_size, obs_size)
    channels = obs_channel[0].reshape(capacity, lat_size, obs_size)
    arrived = (
        lax.all_to_all(
            lax.all_to_all(masked, "lat", split_axis=1, concat_axis=1, tiled=True),
            "obs",
            split_axis=2,
            concat_axis=2,
            tiled=True,
        ),
        lax.all_to_all(
            lax.all_to_all(lat_frac, "lat", split_axis=1, concat_axis=1, tiled=True),
            "obs",
            split_axis=2,
            concat_axis=2,
            tiled=True,
        ),
        lax.all_to_all(
            lax.all_to_all(lon_frac, "lat", split_axis=1, concat_axis=1, tiled=True),
            "obs",
            split_axis=2,
            concat_axis=2,
            tiled=True,
        ),
        lax.all_to_all(
            lax.all_to_all(corners, "lat", split_axis=1, concat_axis=1, tiled=True),
            "obs",
            split_axis=2,
            concat_axis=2,
            tiled=True,
        ),
        lax.all_to_all(
            lax.all_to_all(channels, "lat", split_axis=1, concat_axis=1, tiled=True),
            "obs",
            split_axis=2,
            concat_axis=2,
            tiled=True,
        ),
    )
    chan_base = lax.axis_index("chan") * width
    obs_grad = adjoint_tiles(
        arrived[0],
        arrived[1],
        arrived[2],
        arrived[3],
        arrived[4],
        lat_dev,
        lon_count,
        chan_base,
        width,
    )
    out_grad = next_grad.astype(jnp.float32) + obs_grad
    pre_grad = (out_grad * gelu_slope(pre_act)).astype(jnp.bfloat16)
    longitudes = lax.iota(jnp.int32, lon_count)
    crossed_orders = jnp.transpose(
        order_slots.reshape(lat_size, obs_size, slot_dev), (1, 0, 2)
    ).reshape(total_orders)
    legendre_view = legendre.reshape(slot_dev, degrees, lat_size, obs_size, lat_dev)
    weight_view = quad_weights.reshape(lat_size, obs_size, lat_dev)
    factor = jnp.where(order_slots == 0, 1.0, 2.0).astype(jnp.float32)[:, None]
    cosine, sine = zonal_tables(order_slots, longitudes, lon_count, factor, -factor)
    real_part = jnp.einsum("mn,knc->mkc", cosine, pre_grad, preferred_element_type=jnp.float32)
    imag_part = jnp.einsum("mn,knc->mkc", sine, pre_grad, preferred_element_type=jnp.float32)
    by_order = lax.all_to_all(
        lax.all_to_all(
            jnp.stack([real_part, imag_part], axis=1).astype(jnp.bfloat16),
            "lat",
            split_axis=0,
            concat_axis=2,
            tiled=True,
        ),
        "obs",
        split_axis=0,
        concat_axis=2,
        tiled=True,
    )
    order_view = by_order.reshape(slot_dev, 2, obs_size, lat_size, lat_dev, width)
    up_grad = jnp.einsum(
        "iljka,irkjac->irlc", legendre_view, order_view, preferred_element_type=jnp.float32
    )
    saved = saved_coeffs.astype(jnp.float32)
    gain_terms = jnp.stack(
        [
            jnp.sum(up_grad[:, 0] * saved[:, 0] + up_grad[:, 1] * saved[:, 1], axis=0),
            jnp.sum(up_grad[:, 1] * saved[:, 0] - up_grad[:, 0] * saved[:, 1], axis=0),
        ]
    )
    gain_grad = lax.psum(gain_terms, ("lat", "obs"))
    gain_real = spectral_gain[0]
    gain_imag = spectral_gain[1]
    coeff_grad = jnp.stack(
        [
            gain_real * up_grad[:, 0] + gain_imag * up_grad[:, 1],
            gain_real * up_grad[:, 1] - gain_imag * up_grad[:, 0],
        ],
        axis=1,
    ).astype(jnp.bfloat16)
    analysed = jnp.einsum(
        "iljka,irlc->irjkac", legendre_view, coeff_grad, preferred_element_type=jnp.float32
    )
    lat_grad = (
        (analysed * weight_view[None, None, :, :, :, None])
        .astype(jnp.bfloat16)
        .reshape(slot_dev, 2, lat_count, width)
    )
    by_lat = lax.all_to_all(
        lax.all_to_all(lat_grad, "lat", split_axis=2, concat_axis=0, tiled=True),
        "obs",
        split_axis=2,
        concat_axis=0,
        tiled=True,
    )
    scale = jnp.full((total_orders, 1), 1.0 / lon_count, jnp.float32)
    cosine, sine = zonal_tables(crossed_orders, longitudes, lon_count, scale, -scale)
    spectral_grad = jnp.einsum(
        "mkc,mn->knc", by_lat[:, 0], cosine, preferred_element_type=jnp.float32
    )
    spectral_grad = spectral_grad + jnp.einsum(
        "mkc,mn->knc", by_lat[:, 1], sine, preferred_element_type=jnp.float32
    )
    grid_grad = (out_grad + spectral_grad).astype(jnp.bfloat16)
    return (grid_grad, gain_grad)


CHUNK = 8
F32 = jnp.float32
BF16 = jnp.bfloat16
MESH = pl.DeviceIdType.MESH


def base_tables(order_count, lon_count):
    phase = np.arange(order_count)[:, None] * np.arange(lon_count)[None, :] % lon_count
    angle = phase.astype(np.float32) * np.float32(2.0 * math.pi / lon_count)
    return np.concatenate([np.cos(angle), -np.sin(angle)], axis=1).astype(jnp.bfloat16)


def dot(a, b):
    return jnp.dot(a, b, preferred_element_type=F32)


def block_kernel(
    lat_size,
    obs_size,
    capacity,
    packed,
    order_col,
    order_row,
    quad_col,
    next_hbm,
    act_hbm,
    leg_hbm,
    gain_hbm,
    saved_hbm,
    table_hbm,
    table_t_hbm,
    grid_out,
    gain_out,
    next_ref,
    act_ref,
    leg_ref,
    gain_ref,
    saved_ref,
    table_ref,
    table_t_ref,
    obs_in,
    hot,
    hot_t,
    tab,
    tab_t,
    to_slot,
    to_lat,
    slope_ref,
    out_ref,
    pre_ref,
    fwd_out,
    fwd_in,
    by_slot,
    by_lat,
    bwd_out,
    bwd_in,
    total,
    part_out,
    part_in,
    mine,
    parts,
    local_sem,
    obs_send,
    obs_recv,
    fwd_send,
    fwd_recv,
    bwd_send,
    bwd_recv,
    part_send,
    part_recv,
    full_send,
    full_recv,
):
    group = lat_size * obs_size
    me = lax.axis_index("lat") * obs_size + lax.axis_index("obs")
    lat_dev, lon_count, width = next_ref.shape
    slot_dev, lat_count, degrees = leg_ref.shape
    orders = order_col.shape[0]
    chunks = slot_dev // CHUNK
    rows = CHUNK * lat_dev

    def place(peer):
        return {"lat": peer // obs_size, "obs": peer % obs_size}

    def peers(body):
        def step(j, carry):
            body(lax.rem(me + j, group), lax.rem(me + group - j, group))
            return carry

        lax.fori_loop(1, group, step, 0)

    def send(src, dst, send_sem, recv_sem, peer):
        return pltpu.make_async_remote_copy(
            src_ref=src,
            dst_ref=dst,
            send_sem=send_sem,
            recv_sem=recv_sem,
            device_id=place(peer),
            device_id_type=MESH,
        )

    local = [
        pltpu.make_async_copy(src, dst, local_sem.at[i])
        for i, (src, dst) in enumerate(
            (
                (act_hbm, act_ref),
                (table_hbm, table_ref),
                (next_hbm, next_ref),
                (table_t_hbm, table_t_ref),
                (leg_hbm, leg_ref),
                (gain_hbm, gain_ref),
                (saved_hbm, saved_ref),
            )
        )
    ]
    for copy in local:
        copy.start()

    barrier = pltpu.get_barrier_semaphore()
    peers(
        lambda peer, _: pl.semaphore_signal(
            barrier, inc=1, device_id=place(peer), device_id_type=MESH
        )
    )
    pl.semaphore_wait(barrier, group - 1)

    peers(
        lambda peer, _: send(
            packed.at[peer], obs_in.at[me], obs_send.at[peer], obs_recv.at[me], peer
        ).start()
    )
    obs_in[me] = packed[me]

    local[0].wait()
    for k in range(lat_dev):
        values = act_ref[k].astype(F32)
        cdf = 0.5 * (1.0 + lax.erf(values * 0.7071067811865476))
        density = jnp.exp(-0.5 * values * values) * 0.3989422804014327
        slope_ref[k] = cdf + values * density
    hot[...] = jnp.where(
        lax.broadcasted_iota(jnp.int32, (orders, orders), 1) == order_col[...], 1.0, 0.0
    ).astype(BF16)
    hot_t[...] = jnp.where(
        lax.broadcasted_iota(jnp.int32, (orders, orders), 0) == order_row[...], 1.0, 0.0
    ).astype(BF16)
    side = lat_count * CHUNK
    first = lax.broadcasted_iota(jnp.int32, (side, side), 0)
    second = lax.broadcasted_iota(jnp.int32, (side, side), 1)
    to_lat[...] = jnp.where(
        (first // CHUNK == second % lat_count) & (first % CHUNK == second // lat_count), 1.0, 0.0
    ).astype(BF16)
    to_slot[...] = jnp.where(
        (second // CHUNK == first % lat_count) & (second % CHUNK == first // lat_count), 1.0, 0.0
    ).astype(BF16)
    local[1].wait()
    tile = 256

    for part in range(2):

        def make_tab(i, carry):
            at = pl.multiple_of(i * tile, tile)
            got = dot(hot[...], table_ref[:, pl.ds(part * lon_count + at, tile)]).astype(BF16)
            tab[:, part, :, pl.ds(at, tile)] = got.reshape(chunks, orders // chunks, tile)
            return carry

        lax.fori_loop(0, lon_count // tile, make_tab, 0)

    local[2].wait()
    peers(
        lambda peer, source: send(
            packed.at[peer], obs_in.at[source], obs_send.at[peer], obs_recv.at[source], peer
        ).wait()
    )
    lanes = obs_in.shape[2]
    sources_per = lanes // capacity
    halves = []
    for h in range(group // sources_per):
        halves.append(jnp.sum(obs_in[h * sources_per : (h + 1) * sources_per], axis=0))
    seen = jnp.concatenate(halves, axis=1)
    received = seen.shape[1]
    corner = seen[5:6].astype(jnp.int32)
    channel = seen[6:7].astype(jnp.int32)
    left = corner % lon_count
    right = corner - left + (left + 1) % lon_count
    places = (corner, right, corner + lon_count, right + lon_count)
    chan_ids = lax.axis_index("chan") * width + lax.broadcasted_iota(
        jnp.int32, (width, received), 0
    )
    amounts = jnp.where(chan_ids == channel, seen[0:1], 0.0).astype(BF16)
    for k in range(lat_dev):
        for half in range(2):
            span = lon_count // 2
            begin = half * span
            cells = k * lon_count + begin + lax.broadcasted_iota(jnp.int32, (span, received), 0)
            stencil = jnp.zeros((span, received), F32)
            for w, at in enumerate(places):
                stencil = stencil + jnp.where(cells == at, seen[1 + w : 2 + w], 0.0)
            added = lax.dot_general(
                stencil.astype(BF16), amounts, (((1,), (1,)), ((), ())), preferred_element_type=F32
            )
            here = slice(begin, begin + span)
            out_grad = next_ref[k, here].astype(F32) + added
            out_ref[k, here] = out_grad
            pre_ref[here, k * width : (k + 1) * width] = (out_grad * slope_ref[k, here]).astype(BF16)

    def zonal(q, carry):
        per = orders // chunks
        at = pl.multiple_of(q * per, per)
        factor = jnp.where(order_col[pl.ds(at, per), :] == 0, 1.0, 2.0)
        for part in range(2):
            got = (dot(tab[q, part], pre_ref[...]) * factor).reshape(group, CHUNK, lat_dev * width)
            got = jnp.concatenate(
                [got[:, :, k * width : (k + 1) * width] for k in range(lat_dev)], axis=1
            )
            fwd_out[q, :, :, part * width : (part + 1) * width] = got.astype(BF16)
        fwd_in[q, me] = fwd_out[q, me]
        peers(
            lambda peer, _: send(
                fwd_out.at[q, peer],
                fwd_in.at[q, me],
                fwd_send.at[q, peer],
                fwd_recv.at[q, me],
                peer,
            ).start()
        )
        return carry

    lax.fori_loop(0, chunks, zonal, 0)

    local[3].wait()
    for part in range(2):

        def make_tab_t(i, carry):
            at = pl.multiple_of(i * tile, tile)
            got = dot(table_t_ref[pl.ds(part * lon_count + at, tile), :], hot_t[...])
            tab_t[pl.ds(at, tile), part * orders : (part + 1) * orders] = got.astype(BF16)
            return carry

        lax.fori_loop(0, lon_count // tile, make_tab_t, 0)
    total[...] = jnp.zeros_like(total)
    for copy in local[4:]:
        copy.wait()

    def degrees_of(q, carry):
        peers(
            lambda peer, source: send(
                fwd_out.at[q, peer],
                fwd_in.at[q, source],
                fwd_send.at[q, peer],
                fwd_recv.at[q, source],
                peer,
            ).wait()
        )
        arrived = fwd_in[q].reshape(side, 2 * width)
        by_slot[...] = dot(to_slot[...], arrived).astype(BF16)

        def per_slot(i, inner):
            s = q * CHUNK + i
            at = pl.multiple_of(i * lat_count, lat_count)
            table = leg_ref[s]
            up = lax.dot_general(
                table,
                by_slot[pl.ds(at, lat_count), :],
                (((0,), (0,)), ((), ())),
                preferred_element_type=F32,
            )
            up_real = up[:, :width]
            up_imag = up[:, width:]
            saved_real = saved_ref[s, 0].astype(F32)
            saved_imag = saved_ref[s, 1].astype(F32)
            total[0] += up_real * saved_real + up_imag * saved_imag
            total[1] += up_imag * saved_real - up_real * saved_imag
            gain_real = gain_ref[0]
            gain_imag = gain_ref[1]
            coeff = jnp.concatenate(
                [
                    (gain_real * up_real + gain_imag * up_imag).astype(BF16),
                    (gain_real * up_imag - gain_imag * up_real).astype(BF16),
                ],
                axis=1,
            )
            by_lat[pl.ds(at, lat_count), :] = (dot(table, coeff) * quad_col[...]).astype(BF16)
            return inner

        lax.fori_loop(0, CHUNK, per_slot, 0)
        bwd_out[q] = dot(to_lat[...], by_lat[...]).astype(BF16).reshape(group, rows, 2 * width)
        bwd_in[q, me] = bwd_out[q, me]
        peers(
            lambda peer, _: send(
                bwd_out.at[q, peer],
                bwd_in.at[q, me],
                bwd_send.at[q, peer],
                bwd_recv.at[q, me],
                peer,
            ).start()
        )
        return carry

    lax.fori_loop(0, chunks, degrees_of, 0)

    share = degrees // group
    for r in range(2):
        part_out[:, r * share : (r + 1) * share, :] = (
            total[r].reshape(group, share, width).astype(BF16)
        )
    part_in[me] = part_out[me]
    peers(
        lambda peer, _: send(
            part_out.at[peer], part_in.at[me], part_send.at[peer], part_recv.at[me], peer
        ).start()
    )

    def lat_arrivals(q, carry):
        peers(
            lambda peer, source: send(
                bwd_out.at[q, peer],
                bwd_in.at[q, source],
                bwd_send.at[q, peer],
                bwd_recv.at[q, source],
                peer,
            ).wait()
        )
        return carry

    lax.fori_loop(0, chunks, lat_arrivals, 0)

    peers(
        lambda peer, source: send(
            part_out.at[peer], part_in.at[source], part_send.at[peer], part_recv.at[source], peer
        ).wait()
    )
    mine[...] = jnp.sum(part_in[...].astype(F32), axis=0).astype(BF16)
    parts[me] = mine[...]
    peers(
        lambda peer, _: send(
            mine, parts.at[me], full_send.at[peer], full_recv.at[me], peer
        ).start()
    )

    back = bwd_in[...].astype(F32).reshape(chunks * group, lat_dev, CHUNK, 2 * width)
    pieces = []
    for part in range(2):
        lane = slice(part * width, (part + 1) * width)
        pieces.append(
            jnp.concatenate(
                [back[:, k, :, lane].reshape(orders, width) for k in range(lat_dev)], axis=1
            ).astype(BF16)
        )
    grads = jnp.concatenate(pieces, axis=0)
    pre_ref[0 : 2 * orders, :] = grads

    def to_grid(i, carry):
        at = pl.multiple_of(i * tile, tile)
        got = dot(tab_t[pl.ds(at, tile), :], pre_ref[0 : 2 * orders, :]) * (1.0 / lon_count)
        for k in range(lat_dev):
            grid_out[k, pl.ds(at, tile), :] = (
                out_ref[k, pl.ds(at, tile), :] + got[:, k * width : (k + 1) * width]
            ).astype(BF16)
        return carry

    lax.fori_loop(0, lon_count // tile, to_grid, 0)

    peers(
        lambda peer, source: send(
            mine, parts.at[source], full_send.at[peer], full_recv.at[source], peer
        ).wait()
    )
    for r in range(2):
        gain_out[r] = (
            parts[:, r * share : (r + 1) * share, :].astype(F32).reshape(degrees, width)
        )


def on_device(
    next_grad,
    pre_act,
    legendre,
    order_slots,
    quad_weights,
    spectral_gain,
    saved_coeffs,
    obs_value,
    obs_lat_frac,
    obs_lon_frac,
    obs_corner,
    obs_channel,
    slot_counts,
):
    lat_dev, lon_count, width = next_grad.shape
    lat_size = lax.axis_size("lat")
    obs_size = lax.axis_size("obs")
    group = lat_size * obs_size
    slot_dev, degrees, lat_count = legendre.shape
    orders = order_slots.shape[0]
    capacity = obs_value.shape[1]
    chunks = slot_dev // CHUNK
    rows = CHUNK * lat_dev
    lanes = 128
    side = lat_count * CHUNK

    me = lax.axis_index("lat") * obs_size + lax.axis_index("obs")
    alive_slots = lax.iota(jnp.int32, capacity)[:, None] < slot_counts[0][None, :]
    amounts = jnp.where(alive_slots, obs_value[0], jnp.zeros((), BF16)).astype(F32)
    lat_step = obs_lat_frac[0].astype(F32)
    lon_step = obs_lon_frac[0].astype(F32)
    weights = (
        (1.0 - lat_step) * (1.0 - lon_step),
        (1.0 - lat_step) * lon_step,
        lat_step * (1.0 - lon_step),
        lat_step * lon_step,
    )
    fields = jnp.stack(
        [amounts]
        + [lax.reduce_precision(w, 8, 7) for w in weights]
        + [obs_corner[0].astype(F32), obs_channel[0].astype(F32), jnp.zeros_like(amounts)]
    )
    spots = lanes // capacity
    fields = jnp.transpose(fields, (2, 0, 1))
    packed = jnp.where(
        (lax.iota(jnp.int32, lanes) // capacity == me % spots)[None, None, :],
        jnp.tile(fields, (1, 1, spots)),
        0.0,
    )
    order_q = jnp.transpose(order_slots.reshape(group, chunks, CHUNK), (1, 0, 2)).reshape(orders)
    table = base_tables(orders, lon_count)
    table_t = np.ascontiguousarray(table.T)

    vmem = pl.BlockSpec(memory_space=pltpu.VMEM)
    anywhere = pl.BlockSpec(memory_space=pl.ANY)
    dma = pltpu.SemaphoreType.DMA
    share = degrees // group
    return pl.pallas_call(
        functools.partial(block_kernel, lat_size, obs_size, capacity),
        out_shape=(
            jax.ShapeDtypeStruct((lat_dev, lon_count, width), BF16),
            jax.ShapeDtypeStruct((2, degrees, width), F32),
        ),
        in_specs=[vmem] * 4 + [anywhere] * 7,
        out_specs=(vmem, vmem),
        scratch_shapes=[
            pltpu.VMEM((lat_dev, lon_count, width), BF16),
            pltpu.VMEM((lat_dev, lon_count, width), BF16),
            pltpu.VMEM((slot_dev, lat_count, degrees), BF16),
            pltpu.VMEM((2, degrees, width), F32),
            pltpu.VMEM((slot_dev, 2, degrees, width), BF16),
            pltpu.VMEM((orders, 2 * lon_count), BF16),
            pltpu.VMEM((2 * lon_count, orders), BF16),
            pltpu.VMEM((group, 8, lanes), F32),
            pltpu.VMEM((orders, orders), BF16),
            pltpu.VMEM((orders, orders), BF16),
            pltpu.VMEM((chunks, 2, orders // chunks, lon_count), BF16),
            pltpu.VMEM((lon_count, 2 * orders), BF16),
            pltpu.VMEM((side, side), BF16),
            pltpu.VMEM((side, side), BF16),
            pltpu.VMEM((lat_dev, lon_count, width), F32),
            pltpu.VMEM((lat_dev, lon_count, width), F32),
            pltpu.VMEM((max(lon_count, 2 * orders), lat_dev * width), BF16),
            pltpu.VMEM((chunks, group, rows, 2 * width), BF16),
            pltpu.VMEM((chunks, group, rows, 2 * width), BF16),
            pltpu.VMEM((side, 2 * width), BF16),
            pltpu.VMEM((side, 2 * width), BF16),
            pltpu.VMEM((chunks, group, rows, 2 * width), BF16),
            pltpu.VMEM((chunks, group, rows, 2 * width), BF16),
            pltpu.VMEM((2, degrees, width), F32),
            pltpu.VMEM((group, 2 * share, width), BF16),
            pltpu.VMEM((group, 2 * share, width), BF16),
            pltpu.VMEM((2 * share, width), BF16),
            pltpu.VMEM((group, 2 * share, width), BF16),
            dma((7,)),
            dma((group,)),
            dma((group,)),
            dma((chunks, group)),
            dma((chunks, group)),
            dma((chunks, group)),
            dma((chunks, group)),
            dma((group,)),
            dma((group,)),
            dma((group,)),
            dma((group,)),
        ],
        compiler_params=pltpu.CompilerParams(
            collective_id=0, has_side_effects=True, vmem_limit_bytes=50 * 1024 * 1024
        ),
        name="block_backward",
    )(
        packed,
        order_q[:, None],
        order_q[None, :],
        quad_weights[:, None],
        next_grad,
        pre_act,
        jnp.transpose(legendre, (0, 2, 1)),
        spectral_gain,
        saved_coeffs,
        jnp.asarray(table),
        jnp.asarray(table_t),
    )


def kernel_fits(next_grad, legendre, obs_value, group):
    lat_dev, lon_count, width = next_grad.shape
    slot_dev, degrees, lat_count = legendre.shape
    capacity = obs_value.shape[1]
    return (
        slot_dev % CHUNK == 0
        and (CHUNK * lat_dev) % 16 == 0
        and lat_count * CHUNK <= 512
        and width % 128 == 0
        and lon_count % 512 == 0
        and degrees % (16 * group) == 0
        and 128 % capacity == 0
        and group % (128 // capacity) == 0
    )


def device_path(*args):
    group = lax.axis_size("lat") * lax.axis_size("obs")
    if kernel_fits(args[0], args[2], args[7], group):
        return on_device(*args)
    return plain_path(*args)


def solution(mesh):
    in_specs = (
        P(("lat", "obs"), None, "chan"),
        P(("lat", "obs"), None, "chan"),
        P(("lat", "obs"), None, None),
        P(),
        P(),
        P(None, None, "chan"),
        P(("lat", "obs"), None, None, "chan"),
        P(("lat", "obs"), None, None),
        P(("lat", "obs"), None, None),
        P(("lat", "obs"), None, None),
        P(("lat", "obs"), None, None),
        P(("lat", "obs"), None, None),
        P(("lat", "obs"), None),
    )
    out_specs = (P(("lat", "obs"), None, "chan"), P(None, None, "chan"))
    return jax.shard_map(
        device_path, mesh=mesh, in_specs=in_specs, out_specs=out_specs, check_vma=False
    )
```

```python
import functools
import math

import jax
import jax.numpy as jnp
import numpy as np
from jax import lax
from jax.experimental import pallas as pl
from jax.experimental.pallas import tpu as pltpu
from jax.sharding import PartitionSpec as P


def gelu_slope(pre_act):
    values = pre_act.astype(jnp.float32)
    normal_cdf = 0.5 * (1.0 + jax.scipy.special.erf(values * 0.7071067811865476))
    density = jnp.exp(-0.5 * values * values) * 0.3989422804014327
    return normal_cdf + values * density


def zonal_tables(orders, longitudes, lon_count, cos_weight, sin_weight):
    phase = orders[:, None] * longitudes[None, :] % lon_count
    angle = phase.astype(jnp.float32) * (2.0 * math.pi / lon_count)
    return (
        (cos_weight * jnp.cos(angle)).astype(jnp.bfloat16),
        (sin_weight * jnp.sin(angle)).astype(jnp.bfloat16),
    )


def adjoint_tiles(
    amounts, lat_frac, lon_frac, corners, channels, lat_dev, lon_count, chan_base, width
):
    received = amounts.size
    amounts = amounts.reshape(received)
    lat_frac = lat_frac.reshape(received)
    lon_frac = lon_frac.reshape(received)
    corners = corners.reshape(received)
    channels = channels.reshape(received)
    block_rows = min(512, received)
    cell_ids = lax.iota(jnp.int32, lat_dev * lon_count)
    chan_ids = chan_base + lax.iota(jnp.int32, width)
    nothing = jnp.zeros((), jnp.bfloat16)

    def add_block(counter, summed):
        offset = counter * block_rows
        lat_step = lax.dynamic_slice_in_dim(lat_frac, offset, block_rows).astype(jnp.float32)
        lon_step = lax.dynamic_slice_in_dim(lon_frac, offset, block_rows).astype(jnp.float32)
        corner_ids = lax.dynamic_slice_in_dim(corners, offset, block_rows)
        chan_rows = lax.dynamic_slice_in_dim(channels, offset, block_rows)
        amount_rows = lax.dynamic_slice_in_dim(amounts, offset, block_rows)
        top = corner_ids // lon_count
        left = corner_ids % lon_count
        right = (left + 1) % lon_count
        lower = top * lon_count
        upper = lower + lon_count
        weights = (
            (1.0 - lat_step) * (1.0 - lon_step),
            (1.0 - lat_step) * lon_step,
            lat_step * (1.0 - lon_step),
            lat_step * lon_step,
        )
        places = (lower + left, lower + right, upper + left, upper + right)
        stencil = jnp.zeros((block_rows, lat_dev * lon_count), jnp.bfloat16)
        for weight, place in zip(weights, places):
            stencil = stencil + jnp.where(
                cell_ids[None, :] == place[:, None], weight.astype(jnp.bfloat16)[:, None], nothing
            )
        sources = jnp.where(chan_rows[:, None] == chan_ids[None, :], amount_rows[:, None], nothing)
        return summed + lax.dot_general(
            stencil, sources, (((0,), (0,)), ((), ())), preferred_element_type=jnp.float32
        )

    start_sum = jnp.zeros((lat_dev * lon_count, width), jnp.float32)
    summed = lax.fori_loop(0, received // block_rows, add_block, start_sum)
    return summed.reshape(lat_dev, lon_count, width)


def plain_path(
    next_grad,
    pre_act,
    legendre,
    order_slots,
    quad_weights,
    spectral_gain,
    saved_coeffs,
    obs_value,
    obs_lat_frac,
    obs_lon_frac,
    obs_corner,
    obs_channel,
    slot_counts,
):
    lat_dev, lon_count, width = next_grad.shape
    lat_size = lax.axis_size("lat")
    obs_size = lax.axis_size("obs")
    slot_dev, degrees, lat_count = legendre.shape
    total_orders = order_slots.shape[0]
    capacity = obs_value.shape[1]
    alive_slots = lax.iota(jnp.int32, capacity)[:, None] < slot_counts[0][None, :]
    masked = jnp.where(alive_slots, obs_value[0], jnp.zeros((), jnp.bfloat16)).reshape(
        capacity, lat_size, obs_size
    )
    lat_frac = obs_lat_frac[0].reshape(capacity, lat_size, obs_size)
    lon_frac = obs_lon_frac[0].reshape(capacity, lat_size, obs_size)
    corners = obs_corner[0].reshape(capacity, lat_size, obs_size)
    channels = obs_channel[0].reshape(capacity, lat_size, obs_size)
    arrived = (
        lax.all_to_all(
            lax.all_to_all(masked, "lat", split_axis=1, concat_axis=1, tiled=True),
            "obs",
            split_axis=2,
            concat_axis=2,
            tiled=True,
        ),
        lax.all_to_all(
            lax.all_to_all(lat_frac, "lat", split_axis=1, concat_axis=1, tiled=True),
            "obs",
            split_axis=2,
            concat_axis=2,
            tiled=True,
        ),
        lax.all_to_all(
            lax.all_to_all(lon_frac, "lat", split_axis=1, concat_axis=1, tiled=True),
            "obs",
            split_axis=2,
            concat_axis=2,
            tiled=True,
        ),
        lax.all_to_all(
            lax.all_to_all(corners, "lat", split_axis=1, concat_axis=1, tiled=True),
            "obs",
            split_axis=2,
            concat_axis=2,
            tiled=True,
        ),
        lax.all_to_all(
            lax.all_to_all(channels, "lat", split_axis=1, concat_axis=1, tiled=True),
            "obs",
            split_axis=2,
            concat_axis=2,
            tiled=True,
        ),
    )
    chan_base = lax.axis_index("chan") * width
    obs_grad = adjoint_tiles(
        arrived[0],
        arrived[1],
        arrived[2],
        arrived[3],
        arrived[4],
        lat_dev,
        lon_count,
        chan_base,
        width,
    )
    out_grad = next_grad.astype(jnp.float32) + obs_grad
    pre_grad = (out_grad * gelu_slope(pre_act)).astype(jnp.bfloat16)
    longitudes = lax.iota(jnp.int32, lon_count)
    crossed_orders = jnp.transpose(
        order_slots.reshape(lat_size, obs_size, slot_dev), (1, 0, 2)
    ).reshape(total_orders)
    legendre_view = legendre.reshape(slot_dev, degrees, lat_size, obs_size, lat_dev)
    weight_view = quad_weights.reshape(lat_size, obs_size, lat_dev)
    factor = jnp.where(order_slots == 0, 1.0, 2.0).astype(jnp.float32)[:, None]
    cosine, sine = zonal_tables(order_slots, longitudes, lon_count, factor, -factor)
    real_part = jnp.einsum("mn,knc->mkc", cosine, pre_grad, preferred_element_type=jnp.float32)
    imag_part = jnp.einsum("mn,knc->mkc", sine, pre_grad, preferred_element_type=jnp.float32)
    by_order = lax.all_to_all(
        lax.all_to_all(
            jnp.stack([real_part, imag_part], axis=1).astype(jnp.bfloat16),
            "lat",
            split_axis=0,
            concat_axis=2,
            tiled=True,
        ),
        "obs",
        split_axis=0,
        concat_axis=2,
        tiled=True,
    )
    order_view = by_order.reshape(slot_dev, 2, obs_size, lat_size, lat_dev, width)
    up_grad = jnp.einsum(
        "iljka,irkjac->irlc", legendre_view, order_view, preferred_element_type=jnp.float32
    )
    saved = saved_coeffs.astype(jnp.float32)
    gain_terms = jnp.stack(
        [
            jnp.sum(up_grad[:, 0] * saved[:, 0] + up_grad[:, 1] * saved[:, 1], axis=0),
            jnp.sum(up_grad[:, 1] * saved[:, 0] - up_grad[:, 0] * saved[:, 1], axis=0),
        ]
    )
    gain_grad = lax.psum(gain_terms, ("lat", "obs"))
    gain_real = spectral_gain[0]
    gain_imag = spectral_gain[1]
    coeff_grad = jnp.stack(
        [
            gain_real * up_grad[:, 0] + gain_imag * up_grad[:, 1],
            gain_real * up_grad[:, 1] - gain_imag * up_grad[:, 0],
        ],
        axis=1,
    ).astype(jnp.bfloat16)
    analysed = jnp.einsum(
        "iljka,irlc->irjkac", legendre_view, coeff_grad, preferred_element_type=jnp.float32
    )
    lat_grad = (
        (analysed * weight_view[None, None, :, :, :, None])
        .astype(jnp.bfloat16)
        .reshape(slot_dev, 2, lat_count, width)
    )
    by_lat = lax.all_to_all(
        lax.all_to_all(lat_grad, "lat", split_axis=2, concat_axis=0, tiled=True),
        "obs",
        split_axis=2,
        concat_axis=0,
        tiled=True,
    )
    scale = jnp.full((total_orders, 1), 1.0 / lon_count, jnp.float32)
    cosine, sine = zonal_tables(crossed_orders, longitudes, lon_count, scale, -scale)
    spectral_grad = jnp.einsum(
        "mkc,mn->knc", by_lat[:, 0], cosine, preferred_element_type=jnp.float32
    )
    spectral_grad = spectral_grad + jnp.einsum(
        "mkc,mn->knc", by_lat[:, 1], sine, preferred_element_type=jnp.float32
    )
    grid_grad = (out_grad + spectral_grad).astype(jnp.bfloat16)
    return (grid_grad, gain_grad)


CHUNK = 8
F32 = jnp.float32
BF16 = jnp.bfloat16
MESH = pl.DeviceIdType.MESH


def base_tables(order_count, lon_count):
    phase = np.arange(order_count)[:, None] * np.arange(lon_count)[None, :] % lon_count
    angle = phase.astype(np.float32) * np.float32(2.0 * math.pi / lon_count)
    return np.concatenate([np.cos(angle), -np.sin(angle)], axis=1).astype(jnp.bfloat16)


def dot(a, b):
    return jnp.dot(a, b, preferred_element_type=F32)


def block_kernel(
    lat_size,
    obs_size,
    value_ref,
    lat_frac_ref,
    lon_frac_ref,
    corner_ref,
    channel_ref,
    count_ref,
    order_row,
    quad_row,
    next_hbm,
    act_hbm,
    leg_hbm,
    gain_hbm,
    saved_hbm,
    table_hbm,
    table_t_hbm,
    grid_out,
    gain_out,
    next_ref,
    act_ref,
    leg_ref,
    gain_ref,
    saved_ref,
    table_ref,
    table_t_ref,
    packed,
    obs_in,
    hot,
    hot_t,
    factor_ref,
    tab,
    tab_t,
    leg_t,
    to_slot,
    to_lat,
    slope_ref,
    out_ref,
    pre_ref,
    fwd_out,
    fwd_in,
    by_slot,
    coeff_ref,
    by_lat,
    bwd_out,
    bwd_in,
    total,
    near_out,
    near_in,
    far_out,
    far_in,
    parts,
    local_sem,
    obs_send,
    obs_recv,
    fwd_send,
    fwd_recv,
    bwd_send,
    bwd_recv,
    sum_send,
    sum_recv,
):
    group = lat_size * obs_size
    my_lat = lax.axis_index("lat")
    my_obs = lax.axis_index("obs")
    me = my_lat * obs_size + my_obs
    lat_dev, lon_count, width = next_ref.shape
    slot_dev, lat_count, degrees = leg_ref.shape
    orders = order_row.shape[1]
    capacity = value_ref.shape[1]
    chunks = slot_dev // CHUNK
    rows = CHUNK * lat_dev
    lanes = packed.shape[2]
    tile = 256

    def place(peer):
        return {"lat": peer // obs_size, "obs": peer % obs_size}

    def peers(body):
        def step(j, carry):
            body(lax.rem(me + j, group))
            return carry

        lax.fori_loop(1, group, step, 0)

    def send(src, dst, send_sem, recv_sem, target):
        return pltpu.make_async_remote_copy(
            src_ref=src,
            dst_ref=dst,
            send_sem=send_sem,
            recv_sem=recv_sem,
            device_id=target,
            device_id_type=MESH,
        )

    beside = {"obs": lax.rem(my_obs + 1, obs_size)}

    def iota(shape, axis):
        return lax.broadcasted_iota(jnp.int32, shape, axis)

    def column(row):
        side = row.shape[1]
        same = iota((side, side), 0) == iota((side, side), 1)
        return jnp.sum(jnp.where(same, row, 0.0), axis=1, keepdims=True)

    barrier = pltpu.get_barrier_semaphore()
    peers(
        lambda peer: pl.semaphore_signal(
            barrier, inc=1, device_id=place(peer), device_id_type=MESH
        )
    )
    local = [
        pltpu.make_async_copy(src, dst, local_sem.at[i])
        for i, (src, dst) in enumerate(
            (
                (act_hbm, act_ref),
                (table_hbm, table_ref),
                (next_hbm, next_ref),
                (table_t_hbm, table_t_ref),
                (leg_hbm, leg_ref),
                (gain_hbm, gain_ref),
                (saved_hbm, saved_ref),
            )
        )
    ]
    for copy in local[:3]:
        copy.start()

    alive = iota((capacity, group), 0) < count_ref[...]
    lat_step = lat_frac_ref[0].astype(F32)
    lon_step = lon_frac_ref[0].astype(F32)
    corner = corner_ref[0]
    fields = (
        jnp.where(alive, value_ref[0].astype(F32), 0.0),
        (1.0 - lat_step) * (1.0 - lon_step),
        (1.0 - lat_step) * lon_step,
        lat_step * (1.0 - lon_step),
        lat_step * lon_step,
        (corner // 128).astype(F32),
        (corner % 128).astype(F32),
        channel_ref[0].astype(F32),
    )
    at_row = iota((8 * group, group), 0)
    at_tile = iota((8 * group, group), 1)
    by_row = jnp.zeros((8 * group, capacity), F32)
    for i, field in enumerate(fields):
        pick = jnp.where(at_row == at_tile * 8 + i, 1.0, 0.0).astype(BF16)
        by_row = by_row + lax.dot_general(
            pick, field.astype(BF16), (((1,), (1,)), ((), ())), preferred_element_type=F32
        )
    spots = lanes // capacity
    spread = jnp.where(
        iota((capacity, lanes), 1) == lax.rem(me, spots) * capacity + iota((capacity, lanes), 0),
        1.0,
        0.0,
    ).astype(BF16)
    packed[...] = dot(by_row.astype(BF16), spread).reshape(group, 8, lanes)
    obs_in[me] = packed[me]

    order_f = order_row[...].astype(F32)
    order_col = column(order_f)
    hot[...] = jnp.where(
        iota((orders, orders), 1).astype(F32) == order_col, 1.0, 0.0
    ).astype(BF16)
    hot_t[...] = jnp.where(iota((orders, orders), 0) == order_row[...], 1.0, 0.0).astype(BF16)
    factor = jnp.where(order_col == 0.0, 1.0, 2.0) * jnp.ones((1, lanes), F32)
    factor_ref[...] = jnp.swapaxes(factor.reshape(group, chunks, CHUNK, lanes), 0, 1).reshape(
        chunks, group * CHUNK, lanes
    )

    pl.semaphore_wait(barrier, group - 1)
    peers(
        lambda peer: send(
            packed.at[peer], obs_in.at[me], obs_send, obs_recv, place(peer)
        ).start()
    )
    for copy in local[3:]:
        copy.start()

    local[0].wait()
    for k in range(lat_dev):
        values = act_ref[k].astype(F32)
        cdf = 0.5 * (1.0 + lax.erf(values * 0.7071067811865476))
        density = jnp.exp(-0.5 * values * values) * 0.3989422804014327
        slope_ref[k] = cdf + values * density
    local[1].wait()
    for part in range(2):

        def make_tab(i, carry):
            at = pl.multiple_of(i * tile, tile)
            got = dot(hot[...], table_ref[:, pl.ds(part * lon_count + at, tile)])
            got = jnp.swapaxes(got.reshape(group, chunks, CHUNK, tile), 0, 1)
            tab[:, part, :, pl.ds(at, tile)] = got.reshape(chunks, group * CHUNK, tile).astype(BF16)
            return carry

        lax.fori_loop(0, lon_count // tile, make_tab, 0)

    local[2].wait()
    send(
        packed.at[pl.ds(0, group - 1)],
        obs_in.at[pl.ds(0, group - 1)],
        obs_send,
        obs_recv,
        beside,
    ).wait_recv()
    halves = []
    for h in range(group // spots):
        halves.append(jnp.sum(obs_in[h * spots : (h + 1) * spots], axis=0))
    seen = jnp.concatenate(halves, axis=1)
    received = seen.shape[1]
    corner = seen[5:6].astype(jnp.int32) * 128 + seen[6:7].astype(jnp.int32)
    channel = seen[7:8].astype(jnp.int32)
    left = corner % lon_count
    right = corner - left + (left + 1) % lon_count
    places = (corner, right, corner + lon_count, right + lon_count)
    chan_ids = lax.axis_index("chan") * width + iota((width, received), 0)
    amounts = jnp.where(chan_ids == channel, seen[0:1], 0.0).astype(BF16)
    for k in range(lat_dev):
        for half in range(2):
            span = lon_count // 2
            begin = half * span
            cells = k * lon_count + begin + iota((span, received), 0)
            stencil = jnp.zeros((span, received), F32)
            for w, at in enumerate(places):
                stencil = jnp.where(cells == at, seen[1 + w : 2 + w], stencil)
            added = lax.dot_general(
                stencil.astype(BF16), amounts, (((1,), (1,)), ((), ())), preferred_element_type=F32
            )
            here = slice(begin, begin + span)
            out_grad = next_ref[k, here].astype(F32) + added
            out_ref[k, here] = out_grad
            pre_ref[here, k * width : (k + 1) * width] = (out_grad * slope_ref[k, here]).astype(BF16)

    def zonal(q, carry):
        scale = factor_ref[q][:, 0:1]
        for part in range(2):
            got = (dot(tab[q, part], pre_ref[...]) * scale).reshape(group, CHUNK, lat_dev * width)
            got = jnp.concatenate(
                [got[:, :, k * width : (k + 1) * width] for k in range(lat_dev)], axis=1
            )
            fwd_out[q, :, :, part * width : (part + 1) * width] = got.astype(BF16)
        fwd_in[q, me] = fwd_out[q, me]
        peers(
            lambda peer: send(
                fwd_out.at[q, peer], fwd_in.at[q, me], fwd_send, fwd_recv.at[q], place(peer)
            ).start()
        )
        return carry

    lax.fori_loop(0, chunks, zonal, 0)

    side = lat_count * CHUNK
    first = iota((side, side), 0)
    second = iota((side, side), 1)
    to_lat[...] = jnp.where(
        (first // CHUNK == second % lat_count) & (first % CHUNK == second // lat_count), 1.0, 0.0
    ).astype(BF16)
    to_slot[...] = jnp.where(
        (second // CHUNK == first % lat_count) & (second % CHUNK == first // lat_count), 1.0, 0.0
    ).astype(BF16)
    joined = lanes // lat_count
    for copy in local[4:]:
        copy.wait()

    def turn(j, carry):
        table = leg_ref[pl.ds(j * joined, joined)].reshape(lanes, degrees)
        leg_t[j] = table.T
        return carry

    lax.fori_loop(0, slot_dev // joined, turn, 0)
    total[...] = jnp.zeros_like(total)
    quad = column(quad_row[...])
    local[3].wait()
    for part in range(2):

        def make_tab_t(i, carry):
            at = pl.multiple_of(i * tile, tile)
            got = dot(table_t_ref[pl.ds(part * lon_count + at, tile), :], hot_t[...])
            tab_t[pl.ds(at, tile), part * orders : (part + 1) * orders] = got.astype(BF16)
            return carry

        lax.fori_loop(0, lon_count // tile, make_tab_t, 0)

    span = 128

    def degrees_of(q, carry):
        send(
            fwd_out.at[q, pl.ds(0, group - 1)],
            fwd_in.at[q, pl.ds(0, group - 1)],
            fwd_send,
            fwd_recv.at[q],
            beside,
        ).wait_recv()
        arrived = dot(to_slot[...], fwd_in[q].reshape(side, 2 * width)).astype(BF16)
        owner = iota((lanes, 2 * width), 0) // lat_count
        for i in range(CHUNK):
            begin = i // joined * lanes
            by_slot[i] = jnp.where(
                owner == i % joined, arrived[begin : begin + lanes].astype(F32), 0.0
            ).astype(BF16)

        def degree_tile(t, inner):
            here = pl.ds(pl.multiple_of(t * span, span), span)
            gain_real = gain_ref[0, here, :]
            gain_imag = gain_ref[1, here, :]
            sum_real = total[0, here, :]
            sum_imag = total[1, here, :]
            for i in range(CHUNK):
                s = q * CHUNK + i
                up = dot(leg_t[q * (CHUNK // joined) + i // joined, here, :], by_slot[i])
                up_real = up[:, :width]
                up_imag = up[:, width:]
                saved_real = saved_ref[s, 0, here, :].astype(F32)
                saved_imag = saved_ref[s, 1, here, :].astype(F32)
                sum_real = sum_real + (up_real * saved_real + up_imag * saved_imag)
                sum_imag = sum_imag + (up_imag * saved_real - up_real * saved_imag)
                coeff_ref[i, here, :width] = (
                    gain_real * up_real + gain_imag * up_imag
                ).astype(BF16)
                coeff_ref[i, here, width:] = (
                    gain_real * up_imag - gain_imag * up_real
                ).astype(BF16)
            total[0, here, :] = sum_real
            total[1, here, :] = sum_imag
            return inner

        lax.fori_loop(0, degrees // span, degree_tile, 0)
        for i in range(CHUNK):
            by_lat[i * lat_count : (i + 1) * lat_count, :] = (
                dot(leg_ref[q * CHUNK + i], coeff_ref[i]) * quad
            ).astype(BF16)
        bwd_out[q] = dot(to_lat[...], by_lat[...]).astype(BF16).reshape(group, rows, 2 * width)
        bwd_in[me, q] = bwd_out[q, me]
        peers(
            lambda peer: send(
                bwd_out.at[q, peer], bwd_in.at[me, q], bwd_send, bwd_recv, place(peer)
            ).start()
        )
        return carry

    lax.fori_loop(0, chunks, degrees_of, 0)

    share = degrees // group

    def around(axis, size, mine, src, dst, sem):
        def step(j, carry):
            peer = lax.rem(mine + j, size)
            send(
                src.at[peer],
                dst.at[mine],
                sum_send.at[sem],
                sum_recv.at[sem],
                {axis: peer},
            ).start()
            return carry

        lax.fori_loop(1, size, step, 0)

    def landed(axis, size, mine, src, dst, sem):
        return send(
            src.at[pl.ds(0, size - 1)],
            dst.at[pl.ds(0, size - 1)],
            sum_send.at[sem],
            sum_recv.at[sem],
            {axis: lax.rem(mine + 1, size)},
        )

    stages = (
        ("obs", obs_size, my_obs, near_out, near_in, 0),
        ("lat", lat_size, my_lat, far_out, far_in, 1),
        ("lat", lat_size, my_lat, far_out, far_in, 2),
        ("obs", obs_size, my_obs, parts, parts, 3),
    )
    for r in range(2):
        near_out[:, :, r * share : (r + 1) * share, :] = (
            total[r].reshape(obs_size, lat_size, share, width).astype(BF16)
        )
    near_in[my_obs] = near_out[my_obs]
    around(*stages[0])
    landed(*stages[0]).wait_recv()
    far_out[...] = jnp.sum(near_in[...].astype(F32), axis=0).astype(BF16)
    far_in[my_lat] = far_out[my_lat]
    around(*stages[1])
    landed(*stages[1]).wait_recv()
    parts[my_obs, my_lat] = jnp.sum(far_in[...].astype(F32), axis=0).astype(BF16)

    def spread_out(j, carry):
        peer = lax.rem(my_lat + j, lat_size)
        send(
            parts.at[my_obs, my_lat],
            parts.at[my_obs, my_lat],
            sum_send.at[2],
            sum_recv.at[2],
            {"lat": peer},
        ).start()
        return carry

    lax.fori_loop(1, lat_size, spread_out, 0)

    send(
        bwd_out.at[:, pl.ds(0, group - 1)],
        bwd_in.at[pl.ds(0, group - 1)],
        bwd_send,
        bwd_recv,
        beside,
    ).wait_recv()
    landed(*stages[2]).wait_recv()

    def spread_wide(j, carry):
        send(
            parts.at[my_obs],
            parts.at[my_obs],
            sum_send.at[3],
            sum_recv.at[3],
            {"obs": lax.rem(my_obs + j, obs_size)},
        ).start()
        return carry

    lax.fori_loop(1, obs_size, spread_wide, 0)

    back = bwd_in[...].astype(F32).reshape(group * chunks, lat_dev, CHUNK, 2 * width)
    for part in range(2):
        lane = slice(part * width, (part + 1) * width)
        pre_ref[part * orders : (part + 1) * orders, :] = jnp.concatenate(
            [back[:, k, :, lane].reshape(orders, width) for k in range(lat_dev)], axis=1
        ).astype(BF16)

    def to_grid(i, carry):
        at = pl.multiple_of(i * tile, tile)
        got = dot(tab_t[pl.ds(at, tile), :], pre_ref[0 : 2 * orders, :]) * (1.0 / lon_count)
        for k in range(lat_dev):
            grid_out[k, pl.ds(at, tile), :] = (
                out_ref[k, pl.ds(at, tile), :] + got[:, k * width : (k + 1) * width]
            ).astype(BF16)
        return carry

    lax.fori_loop(0, lon_count // tile, to_grid, 0)

    landed(*stages[3]).wait_recv()
    for r in range(2):
        gain_out[r] = (
            parts[:, :, r * share : (r + 1) * share, :].astype(F32).reshape(degrees, width)
        )

    send(
        packed.at[pl.ds(0, group - 1)], obs_in.at[pl.ds(0, group - 1)], obs_send, obs_recv, beside
    ).wait_send()
    send(
        fwd_out.at[:, pl.ds(0, group - 1)],
        fwd_in.at[:, pl.ds(0, group - 1)],
        fwd_send,
        fwd_recv.at[0],
        beside,
    ).wait_send()
    send(
        bwd_out.at[:, pl.ds(0, group - 1)],
        bwd_in.at[pl.ds(0, group - 1)],
        bwd_send,
        bwd_recv,
        beside,
    ).wait_send()
    landed(*stages[0]).wait_send()
    landed(*stages[1]).wait_send()
    landed(*stages[2]).wait_send()
    landed(*stages[3]).wait_send()


def on_device(
    next_grad,
    pre_act,
    legendre,
    order_slots,
    quad_weights,
    spectral_gain,
    saved_coeffs,
    obs_value,
    obs_lat_frac,
    obs_lon_frac,
    obs_corner,
    obs_channel,
    slot_counts,
):
    lat_dev, lon_count, width = next_grad.shape
    lat_size = lax.axis_size("lat")
    obs_size = lax.axis_size("obs")
    group = lat_size * obs_size
    slot_dev, degrees, lat_count = legendre.shape
    orders = order_slots.shape[0]
    chunks = slot_dev // CHUNK
    rows = CHUNK * lat_dev
    lanes = 128
    side = lat_count * CHUNK
    joined = lanes // lat_count
    table = base_tables(orders, lon_count)
    table_t = np.ascontiguousarray(table.T)

    vmem = pl.BlockSpec(memory_space=pltpu.VMEM)
    anywhere = pl.BlockSpec(memory_space=pl.ANY)
    dma = pltpu.SemaphoreType.DMA
    share = degrees // group
    return pl.pallas_call(
        functools.partial(block_kernel, lat_size, obs_size),
        out_shape=(
            jax.ShapeDtypeStruct((lat_dev, lon_count, width), BF16),
            jax.ShapeDtypeStruct((2, degrees, width), F32),
        ),
        in_specs=[vmem] * 8 + [anywhere] * 7,
        out_specs=(vmem, vmem),
        scratch_shapes=[
            pltpu.VMEM((lat_dev, lon_count, width), BF16),
            pltpu.VMEM((lat_dev, lon_count, width), BF16),
            pltpu.VMEM((slot_dev, lat_count, degrees), BF16),
            pltpu.VMEM((2, degrees, width), F32),
            pltpu.VMEM((slot_dev, 2, degrees, width), BF16),
            pltpu.VMEM((orders, 2 * lon_count), BF16),
            pltpu.VMEM((2 * lon_count, orders), BF16),
            pltpu.VMEM((group, 8, lanes), F32),
            pltpu.VMEM((group, 8, lanes), F32),
            pltpu.VMEM((orders, orders), BF16),
            pltpu.VMEM((orders, orders), BF16),
            pltpu.VMEM((chunks, group * CHUNK, lanes), F32),
            pltpu.VMEM((chunks, 2, orders // chunks, lon_count), BF16),
            pltpu.VMEM((lon_count, 2 * orders), BF16),
            pltpu.VMEM((slot_dev // joined, degrees, lanes), BF16),
            pltpu.VMEM((side, side), BF16),
            pltpu.VMEM((side, side), BF16),
            pltpu.VMEM((lat_dev, lon_count, width), F32),
            pltpu.VMEM((lat_dev, lon_count, width), F32),
            pltpu.VMEM((max(lon_count, 2 * orders), lat_dev * width), BF16),
            pltpu.VMEM((chunks, group, rows, 2 * width), BF16),
            pltpu.VMEM((chunks, group, rows, 2 * width), BF16),
            pltpu.VMEM((CHUNK, lanes, 2 * width), BF16),
            pltpu.VMEM((CHUNK, degrees, 2 * width), BF16),
            pltpu.VMEM((side, 2 * width), BF16),
            pltpu.VMEM((chunks, group, rows, 2 * width), BF16),
            pltpu.VMEM((group, chunks, rows, 2 * width), BF16),
            pltpu.VMEM((2, degrees, width), F32),
            pltpu.VMEM((obs_size, lat_size, 2 * share, width), BF16),
            pltpu.VMEM((obs_size, lat_size, 2 * share, width), BF16),
            pltpu.VMEM((lat_size, 2 * share, width), BF16),
            pltpu.VMEM((lat_size, 2 * share, width), BF16),
            pltpu.VMEM((obs_size, lat_size, 2 * share, width), BF16),
            dma((7,)),
            dma,
            dma,
            dma,
            dma((chunks,)),
            dma,
            dma,
            dma((4,)),
            dma((4,)),
        ],
        compiler_params=pltpu.CompilerParams(
            collective_id=0, has_side_effects=True, vmem_limit_bytes=60 * 1024 * 1024
        ),
        name="block_backward",
    )(
        obs_value,
        obs_lat_frac,
        obs_lon_frac,
        obs_corner,
        obs_channel,
        slot_counts,
        order_slots[None, :],
        quad_weights[None, :],
        next_grad,
        pre_act,
        jnp.transpose(legendre, (0, 2, 1)),
        spectral_gain,
        saved_coeffs,
        jnp.asarray(table),
        jnp.asarray(table_t),
    )


def kernel_fits(next_grad, legendre, obs_value, lat_size, obs_size):
    group = lat_size * obs_size
    lat_dev, lon_count, width = next_grad.shape
    slot_dev, degrees, lat_count = legendre.shape
    capacity = obs_value.shape[1]
    return (
        slot_dev % CHUNK == 0
        and (CHUNK * lat_dev) % 16 == 0
        and lat_count * CHUNK <= 512
        and 128 % lat_count == 0
        and CHUNK % (128 // lat_count) == 0
        and degrees % 128 == 0
        and lat_size > 1
        and obs_size > 1
        and width % 128 == 0
        and lon_count % 512 == 0
        and degrees % (16 * group) == 0
        and 128 % capacity == 0
        and group % (128 // capacity) == 0
    )


def device_path(*args):
    if kernel_fits(args[0], args[2], args[7], lax.axis_size("lat"), lax.axis_size("obs")):
        return on_device(*args)
    return plain_path(*args)


def solution(mesh):
    in_specs = (
        P(("lat", "obs"), None, "chan"),
        P(("lat", "obs"), None, "chan"),
        P(("lat", "obs"), None, None),
        P(),
        P(),
        P(None, None, "chan"),
        P(("lat", "obs"), None, None, "chan"),
        P(("lat", "obs"), None, None),
        P(("lat", "obs"), None, None),
        P(("lat", "obs"), None, None),
        P(("lat", "obs"), None, None),
        P(("lat", "obs"), None, None),
        P(("lat", "obs"), None),
    )
    out_specs = (P(("lat", "obs"), None, "chan"), P(None, None, "chan"))
    return jax.shard_map(
        device_path, mesh=mesh, in_specs=in_specs, out_specs=out_specs, check_vma=False
    )
```

```python
import functools
import math

import jax
import jax.numpy as jnp
import numpy as np
from jax import lax
from jax.experimental import pallas as pl
from jax.experimental.pallas import tpu as pltpu
from jax.sharding import PartitionSpec as P


def gelu_slope(pre_act):
    values = pre_act.astype(jnp.float32)
    normal_cdf = 0.5 * (1.0 + jax.scipy.special.erf(values * 0.7071067811865476))
    density = jnp.exp(-0.5 * values * values) * 0.3989422804014327
    return normal_cdf + values * density


def zonal_tables(orders, longitudes, lon_count, cos_weight, sin_weight):
    phase = orders[:, None] * longitudes[None, :] % lon_count
    angle = phase.astype(jnp.float32) * (2.0 * math.pi / lon_count)
    return (
        (cos_weight * jnp.cos(angle)).astype(jnp.bfloat16),
        (sin_weight * jnp.sin(angle)).astype(jnp.bfloat16),
    )


def adjoint_tiles(
    amounts, lat_frac, lon_frac, corners, channels, lat_dev, lon_count, chan_base, width
):
    received = amounts.size
    amounts = amounts.reshape(received)
    lat_frac = lat_frac.reshape(received)
    lon_frac = lon_frac.reshape(received)
    corners = corners.reshape(received)
    channels = channels.reshape(received)
    block_rows = min(512, received)
    cell_ids = lax.iota(jnp.int32, lat_dev * lon_count)
    chan_ids = chan_base + lax.iota(jnp.int32, width)
    nothing = jnp.zeros((), jnp.bfloat16)

    def add_block(counter, summed):
        offset = counter * block_rows
        lat_step = lax.dynamic_slice_in_dim(lat_frac, offset, block_rows).astype(jnp.float32)
        lon_step = lax.dynamic_slice_in_dim(lon_frac, offset, block_rows).astype(jnp.float32)
        corner_ids = lax.dynamic_slice_in_dim(corners, offset, block_rows)
        chan_rows = lax.dynamic_slice_in_dim(channels, offset, block_rows)
        amount_rows = lax.dynamic_slice_in_dim(amounts, offset, block_rows)
        top = corner_ids // lon_count
        left = corner_ids % lon_count
        right = (left + 1) % lon_count
        lower = top * lon_count
        upper = lower + lon_count
        weights = (
            (1.0 - lat_step) * (1.0 - lon_step),
            (1.0 - lat_step) * lon_step,
            lat_step * (1.0 - lon_step),
            lat_step * lon_step,
        )
        places = (lower + left, lower + right, upper + left, upper + right)
        stencil = jnp.zeros((block_rows, lat_dev * lon_count), jnp.bfloat16)
        for weight, place in zip(weights, places):
            stencil = stencil + jnp.where(
                cell_ids[None, :] == place[:, None], weight.astype(jnp.bfloat16)[:, None], nothing
            )
        sources = jnp.where(chan_rows[:, None] == chan_ids[None, :], amount_rows[:, None], nothing)
        return summed + lax.dot_general(
            stencil, sources, (((0,), (0,)), ((), ())), preferred_element_type=jnp.float32
        )

    start_sum = jnp.zeros((lat_dev * lon_count, width), jnp.float32)
    summed = lax.fori_loop(0, received // block_rows, add_block, start_sum)
    return summed.reshape(lat_dev, lon_count, width)


def plain_path(
    next_grad,
    pre_act,
    legendre,
    order_slots,
    quad_weights,
    spectral_gain,
    saved_coeffs,
    obs_value,
    obs_lat_frac,
    obs_lon_frac,
    obs_corner,
    obs_channel,
    slot_counts,
):
    lat_dev, lon_count, width = next_grad.shape
    lat_size = lax.axis_size("lat")
    obs_size = lax.axis_size("obs")
    slot_dev, degrees, lat_count = legendre.shape
    total_orders = order_slots.shape[0]
    capacity = obs_value.shape[1]
    alive_slots = lax.iota(jnp.int32, capacity)[:, None] < slot_counts[0][None, :]
    masked = jnp.where(alive_slots, obs_value[0], jnp.zeros((), jnp.bfloat16)).reshape(
        capacity, lat_size, obs_size
    )
    lat_frac = obs_lat_frac[0].reshape(capacity, lat_size, obs_size)
    lon_frac = obs_lon_frac[0].reshape(capacity, lat_size, obs_size)
    corners = obs_corner[0].reshape(capacity, lat_size, obs_size)
    channels = obs_channel[0].reshape(capacity, lat_size, obs_size)
    arrived = (
        lax.all_to_all(
            lax.all_to_all(masked, "lat", split_axis=1, concat_axis=1, tiled=True),
            "obs",
            split_axis=2,
            concat_axis=2,
            tiled=True,
        ),
        lax.all_to_all(
            lax.all_to_all(lat_frac, "lat", split_axis=1, concat_axis=1, tiled=True),
            "obs",
            split_axis=2,
            concat_axis=2,
            tiled=True,
        ),
        lax.all_to_all(
            lax.all_to_all(lon_frac, "lat", split_axis=1, concat_axis=1, tiled=True),
            "obs",
            split_axis=2,
            concat_axis=2,
            tiled=True,
        ),
        lax.all_to_all(
            lax.all_to_all(corners, "lat", split_axis=1, concat_axis=1, tiled=True),
            "obs",
            split_axis=2,
            concat_axis=2,
            tiled=True,
        ),
        lax.all_to_all(
            lax.all_to_all(channels, "lat", split_axis=1, concat_axis=1, tiled=True),
            "obs",
            split_axis=2,
            concat_axis=2,
            tiled=True,
        ),
    )
    chan_base = lax.axis_index("chan") * width
    obs_grad = adjoint_tiles(
        arrived[0],
        arrived[1],
        arrived[2],
        arrived[3],
        arrived[4],
        lat_dev,
        lon_count,
        chan_base,
        width,
    )
    out_grad = next_grad.astype(jnp.float32) + obs_grad
    pre_grad = (out_grad * gelu_slope(pre_act)).astype(jnp.bfloat16)
    longitudes = lax.iota(jnp.int32, lon_count)
    crossed_orders = jnp.transpose(
        order_slots.reshape(lat_size, obs_size, slot_dev), (1, 0, 2)
    ).reshape(total_orders)
    legendre_view = legendre.reshape(slot_dev, degrees, lat_size, obs_size, lat_dev)
    weight_view = quad_weights.reshape(lat_size, obs_size, lat_dev)
    factor = jnp.where(order_slots == 0, 1.0, 2.0).astype(jnp.float32)[:, None]
    cosine, sine = zonal_tables(order_slots, longitudes, lon_count, factor, -factor)
    real_part = jnp.einsum("mn,knc->mkc", cosine, pre_grad, preferred_element_type=jnp.float32)
    imag_part = jnp.einsum("mn,knc->mkc", sine, pre_grad, preferred_element_type=jnp.float32)
    by_order = lax.all_to_all(
        lax.all_to_all(
            jnp.stack([real_part, imag_part], axis=1).astype(jnp.bfloat16),
            "lat",
            split_axis=0,
            concat_axis=2,
            tiled=True,
        ),
        "obs",
        split_axis=0,
        concat_axis=2,
        tiled=True,
    )
    order_view = by_order.reshape(slot_dev, 2, obs_size, lat_size, lat_dev, width)
    up_grad = jnp.einsum(
        "iljka,irkjac->irlc", legendre_view, order_view, preferred_element_type=jnp.float32
    )
    saved = saved_coeffs.astype(jnp.float32)
    gain_terms = jnp.stack(
        [
            jnp.sum(up_grad[:, 0] * saved[:, 0] + up_grad[:, 1] * saved[:, 1], axis=0),
            jnp.sum(up_grad[:, 1] * saved[:, 0] - up_grad[:, 0] * saved[:, 1], axis=0),
        ]
    )
    gain_grad = lax.psum(gain_terms, ("lat", "obs"))
    gain_real = spectral_gain[0]
    gain_imag = spectral_gain[1]
    coeff_grad = jnp.stack(
        [
            gain_real * up_grad[:, 0] + gain_imag * up_grad[:, 1],
            gain_real * up_grad[:, 1] - gain_imag * up_grad[:, 0],
        ],
        axis=1,
    ).astype(jnp.bfloat16)
    analysed = jnp.einsum(
        "iljka,irlc->irjkac", legendre_view, coeff_grad, preferred_element_type=jnp.float32
    )
    lat_grad = (
        (analysed * weight_view[None, None, :, :, :, None])
        .astype(jnp.bfloat16)
        .reshape(slot_dev, 2, lat_count, width)
    )
    by_lat = lax.all_to_all(
        lax.all_to_all(lat_grad, "lat", split_axis=2, concat_axis=0, tiled=True),
        "obs",
        split_axis=2,
        concat_axis=0,
        tiled=True,
    )
    scale = jnp.full((total_orders, 1), 1.0 / lon_count, jnp.float32)
    cosine, sine = zonal_tables(crossed_orders, longitudes, lon_count, scale, -scale)
    spectral_grad = jnp.einsum(
        "mkc,mn->knc", by_lat[:, 0], cosine, preferred_element_type=jnp.float32
    )
    spectral_grad = spectral_grad + jnp.einsum(
        "mkc,mn->knc", by_lat[:, 1], sine, preferred_element_type=jnp.float32
    )
    grid_grad = (out_grad + spectral_grad).astype(jnp.bfloat16)
    return (grid_grad, gain_grad)


CHUNK = 8
F32 = jnp.float32
BF16 = jnp.bfloat16
MESH = pl.DeviceIdType.MESH


def base_tables(order_count, lon_count):
    phase = np.arange(order_count)[:, None] * np.arange(lon_count)[None, :] % lon_count
    angle = phase.astype(np.float32) * np.float32(2.0 * math.pi / lon_count)
    return np.concatenate([np.cos(angle), -np.sin(angle)], axis=1).astype(jnp.bfloat16)


def dot(a, b):
    return jnp.dot(a, b, preferred_element_type=F32)


def block_kernel(
    lat_size,
    obs_size,
    value_ref,
    lat_frac_ref,
    lon_frac_ref,
    corner_ref,
    channel_ref,
    count_ref,
    order_row,
    quad_row,
    next_hbm,
    act_hbm,
    leg_hbm,
    gain_hbm,
    saved_hbm,
    table_hbm,
    table_t_hbm,
    grid_out,
    gain_out,
    next_ref,
    act_ref,
    leg_ref,
    gain_ref,
    saved_ref,
    table_ref,
    table_t_ref,
    packed,
    obs_in,
    hot,
    hot_t,
    waves,
    tab_t,
    leg_t,
    to_slot,
    to_lat,
    slope_ref,
    out_ref,
    pre_ref,
    fwd_out,
    fwd_in,
    by_slot,
    coeff_ref,
    by_lat,
    bwd_out,
    bwd_in,
    total,
    near_out,
    near_in,
    far_out,
    far_in,
    parts,
    local_sem,
    obs_send,
    obs_recv,
    fwd_send,
    fwd_recv,
    bwd_send,
    bwd_recv,
    sum_send,
    sum_recv,
):
    group = lat_size * obs_size
    my_lat = lax.axis_index("lat")
    my_obs = lax.axis_index("obs")
    me = my_lat * obs_size + my_obs
    lat_dev, lon_count, width = next_ref.shape
    slot_dev, lat_count, degrees = leg_ref.shape
    orders = order_row.shape[1]
    capacity = value_ref.shape[1]
    chunks = slot_dev // CHUNK
    rows = CHUNK * lat_dev
    lanes = packed.shape[2]
    tile = 256

    others = []
    for j in range(1, group):
        lat_at = lax.rem(my_lat + j // obs_size, lat_size)
        obs_at = lax.rem(my_obs + j % obs_size, obs_size)
        others.append((lat_at * obs_size + obs_at, {"lat": lat_at, "obs": obs_at}))

    def peers(body):
        for peer, where in others:
            body(peer, where)

    def send(src, dst, send_sem, recv_sem, target):
        return pltpu.make_async_remote_copy(
            src_ref=src,
            dst_ref=dst,
            send_sem=send_sem,
            recv_sem=recv_sem,
            device_id=target,
            device_id_type=MESH,
        )

    beside = {"obs": lax.rem(my_obs + 1, obs_size)}

    def iota(shape, axis):
        return lax.broadcasted_iota(jnp.int32, shape, axis)

    def column(row):
        side = row.shape[1]
        same = iota((side, side), 0) == iota((side, side), 1)
        return jnp.sum(jnp.where(same, row, 0.0), axis=1, keepdims=True)

    barrier = pltpu.get_barrier_semaphore()
    peers(
        lambda _, where: pl.semaphore_signal(
            barrier, inc=1, device_id=where, device_id_type=MESH
        )
    )
    local = [
        pltpu.make_async_copy(src, dst, local_sem.at[i])
        for i, (src, dst) in enumerate(
            (
                (act_hbm, act_ref),
                (table_hbm, table_ref),
                (next_hbm, next_ref),
                (table_t_hbm, table_t_ref),
                (leg_hbm, leg_ref),
                (gain_hbm, gain_ref),
                (saved_hbm, saved_ref),
            )
        )
    ]
    for copy in local[:3]:
        copy.start()

    alive = iota((capacity, group), 0) < count_ref[...]
    lat_step = lat_frac_ref[0].astype(F32)
    lon_step = lon_frac_ref[0].astype(F32)
    corner = corner_ref[0]
    fields = (
        jnp.where(alive, value_ref[0].astype(F32), 0.0),
        (1.0 - lat_step) * (1.0 - lon_step),
        (1.0 - lat_step) * lon_step,
        lat_step * (1.0 - lon_step),
        lat_step * lon_step,
        (corner // 128).astype(F32),
        (corner % 128).astype(F32),
        channel_ref[0].astype(F32),
    )
    at_row = iota((8 * group, group), 0)
    at_tile = iota((8 * group, group), 1)
    by_row = jnp.zeros((8 * group, capacity), F32)
    for i, field in enumerate(fields):
        pick = jnp.where(at_row == at_tile * 8 + i, 1.0, 0.0).astype(BF16)
        by_row = by_row + lax.dot_general(
            pick, field.astype(BF16), (((1,), (1,)), ((), ())), preferred_element_type=F32
        )
    spots = lanes // capacity
    spread = jnp.where(
        iota((capacity, lanes), 1) == lax.rem(me, spots) * capacity + iota((capacity, lanes), 0),
        1.0,
        0.0,
    ).astype(BF16)
    packed[...] = dot(by_row.astype(BF16), spread).reshape(group, 8, lanes)
    obs_in[me] = packed[me]

    order_f = order_row[...].astype(F32)
    order_col = column(order_f).reshape(group, chunks, CHUNK, 1)
    per = orders // chunks
    for q in range(chunks):
        here = order_col[:, q].reshape(per, 1)
        hot[q] = jnp.where(iota((per, orders), 1).astype(F32) == here, 1.0, 0.0).astype(BF16)

    pl.semaphore_wait(barrier, group - 1)
    peers(
        lambda peer, where: send(
            packed.at[peer], obs_in.at[me], obs_send, obs_recv, where
        ).start()
    )
    for copy in local[3:]:
        copy.start()

    local[0].wait()
    for k in range(lat_dev):
        values = act_ref[k].astype(F32)
        cdf = 0.5 * (1.0 + lax.erf(values * 0.7071067811865476))
        density = jnp.exp(-0.5 * values * values) * 0.3989422804014327
        slope_ref[k] = cdf + values * density
    local[2].wait()
    send(
        packed.at[pl.ds(0, group - 1)],
        obs_in.at[pl.ds(0, group - 1)],
        obs_send,
        obs_recv,
        beside,
    ).wait_recv()
    halves = []
    for h in range(group // spots):
        halves.append(jnp.sum(obs_in[h * spots : (h + 1) * spots], axis=0))
    seen = jnp.concatenate(halves, axis=1)
    received = seen.shape[1]
    corner = seen[5:6].astype(jnp.int32) * 128 + seen[6:7].astype(jnp.int32)
    channel = seen[7:8].astype(jnp.int32)
    left = corner % lon_count
    right = corner - left + (left + 1) % lon_count
    places = (corner, right, corner + lon_count, right + lon_count)
    chan_ids = lax.axis_index("chan") * width + iota((width, received), 0)
    amounts = jnp.where(chan_ids == channel, seen[0:1], 0.0).astype(BF16)
    for k in range(lat_dev):
        for half in range(2):
            span = lon_count // 2
            begin = half * span
            cells = k * lon_count + begin + iota((span, received), 0)
            stencil = jnp.zeros((span, received), F32)
            for w, at in enumerate(places):
                stencil = jnp.where(cells == at, seen[1 + w : 2 + w], stencil)
            added = lax.dot_general(
                stencil.astype(BF16), amounts, (((1,), (1,)), ((), ())), preferred_element_type=F32
            )
            here = slice(begin, begin + span)
            out_grad = next_ref[k, here].astype(F32) + added
            out_ref[k, here] = out_grad
            pre_ref[here, k * width : (k + 1) * width] = (out_grad * slope_ref[k, here]).astype(BF16)

    local[1].wait()
    factor = jnp.where(iota((orders, 1), 0) == 0, 1.0, 2.0)
    for part in range(2):
        got = dot(table_ref[:, part * lon_count : (part + 1) * lon_count], pre_ref[...])
        for k in range(lat_dev):
            begin = (k * 2 + part) * width
            waves[:, begin : begin + width] = (
                got[:, k * width : (k + 1) * width] * factor
            ).astype(BF16)

    def zonal(q, carry):
        got = dot(hot[q], waves[...]).reshape(group, CHUNK, lat_dev * 2 * width)
        fwd_out[q] = jnp.concatenate(
            [got[:, :, k * 2 * width : (k + 1) * 2 * width] for k in range(lat_dev)], axis=1
        ).astype(BF16)
        fwd_in[q, me] = fwd_out[q, me]
        peers(
            lambda peer, where: send(
                fwd_out.at[q, peer], fwd_in.at[q, me], fwd_send, fwd_recv.at[q], where
            ).start()
        )
        return carry

    lax.fori_loop(0, chunks, zonal, 0)

    side = lat_count * CHUNK
    first = iota((side, side), 0)
    second = iota((side, side), 1)
    to_lat[...] = jnp.where(
        (first // CHUNK == second % lat_count) & (first % CHUNK == second // lat_count), 1.0, 0.0
    ).astype(BF16)
    to_slot[...] = jnp.where(
        (second // CHUNK == first % lat_count) & (second % CHUNK == first // lat_count), 1.0, 0.0
    ).astype(BF16)
    joined = lanes // lat_count
    for copy in local[4:]:
        copy.wait()

    def turn(j, carry):
        table = leg_ref[pl.ds(j * joined, joined)].reshape(lanes, degrees)
        leg_t[j] = table.T
        return carry

    lax.fori_loop(0, slot_dev // joined, turn, 0)
    total[...] = jnp.zeros_like(total)
    quad = column(quad_row[...])

    def make_tab_t(part):
        def step(i, carry):
            at = pl.multiple_of(i * tile, tile)
            got = dot(table_t_ref[pl.ds(part * lon_count + at, tile), :], hot_t[...])
            tab_t[pl.ds(at, tile), part * orders : (part + 1) * orders] = got.astype(BF16)
            return carry

        lax.fori_loop(0, lon_count // tile, step, 0)

    span = 128

    def degrees_of(q, carry):
        send(
            fwd_out.at[q, pl.ds(0, group - 1)],
            fwd_in.at[q, pl.ds(0, group - 1)],
            fwd_send,
            fwd_recv.at[q],
            beside,
        ).wait_recv()
        arrived = dot(to_slot[...], fwd_in[q].reshape(side, 2 * width)).astype(BF16)
        owner = iota((lanes, 2 * width), 0) // lat_count
        for i in range(CHUNK):
            begin = i // joined * lanes
            by_slot[i] = jnp.where(
                owner == i % joined, arrived[begin : begin + lanes].astype(F32), 0.0
            ).astype(BF16)

        def degree_tile(t, inner):
            here = pl.ds(pl.multiple_of(t * span, span), span)
            gain_real = gain_ref[0, here, :]
            gain_imag = gain_ref[1, here, :]
            sum_real = total[0, here, :]
            sum_imag = total[1, here, :]
            for i in range(CHUNK):
                s = q * CHUNK + i
                up = dot(leg_t[q * (CHUNK // joined) + i // joined, here, :], by_slot[i])
                up_real = up[:, :width]
                up_imag = up[:, width:]
                saved_real = saved_ref[s, 0, here, :].astype(F32)
                saved_imag = saved_ref[s, 1, here, :].astype(F32)
                sum_real = sum_real + (up_real * saved_real + up_imag * saved_imag)
                sum_imag = sum_imag + (up_imag * saved_real - up_real * saved_imag)
                coeff_ref[i, here, :width] = (
                    gain_real * up_real + gain_imag * up_imag
                ).astype(BF16)
                coeff_ref[i, here, width:] = (
                    gain_real * up_imag - gain_imag * up_real
                ).astype(BF16)
            total[0, here, :] = sum_real
            total[1, here, :] = sum_imag
            return inner

        lax.fori_loop(0, degrees // span, degree_tile, 0)
        for i in range(CHUNK):
            by_lat[i * lat_count : (i + 1) * lat_count, :] = (
                dot(leg_ref[q * CHUNK + i], coeff_ref[i]) * quad
            ).astype(BF16)
        bwd_out[q] = dot(to_lat[...], by_lat[...]).astype(BF16).reshape(group, rows, 2 * width)
        bwd_in[me, q] = bwd_out[q, me]
        peers(
            lambda peer, where: send(
                bwd_out.at[q, peer], bwd_in.at[me, q], bwd_send, bwd_recv, where
            ).start()
        )
        return carry

    lax.fori_loop(0, chunks, degrees_of, 0)

    share = degrees // group

    def around(axis, size, mine, src, dst, sem):
        def step(j, carry):
            peer = lax.rem(mine + j, size)
            send(
                src.at[peer],
                dst.at[mine],
                sum_send.at[sem],
                sum_recv.at[sem],
                {axis: peer},
            ).start()
            return carry

        lax.fori_loop(1, size, step, 0)

    def landed(axis, size, mine, src, dst, sem):
        return send(
            src.at[pl.ds(0, size - 1)],
            dst.at[pl.ds(0, size - 1)],
            sum_send.at[sem],
            sum_recv.at[sem],
            {axis: lax.rem(mine + 1, size)},
        )

    stages = (
        ("obs", obs_size, my_obs, near_out, near_in, 0),
        ("lat", lat_size, my_lat, far_out, far_in, 1),
        ("lat", lat_size, my_lat, far_out, far_in, 2),
        ("obs", obs_size, my_obs, parts, parts, 3),
    )
    for r in range(2):
        near_out[:, :, r * share : (r + 1) * share, :] = (
            total[r].reshape(obs_size, lat_size, share, width).astype(BF16)
        )
    near_in[my_obs] = near_out[my_obs]
    around(*stages[0])
    hot_t[...] = jnp.where(iota((orders, orders), 0) == order_row[...], 1.0, 0.0).astype(BF16)
    local[3].wait()
    make_tab_t(0)
    landed(*stages[0]).wait_recv()
    far_out[...] = jnp.sum(near_in[...].astype(F32), axis=0).astype(BF16)
    far_in[my_lat] = far_out[my_lat]
    around(*stages[1])
    make_tab_t(1)
    landed(*stages[1]).wait_recv()
    parts[my_obs, my_lat] = jnp.sum(far_in[...].astype(F32), axis=0).astype(BF16)

    def spread_out(j, carry):
        peer = lax.rem(my_lat + j, lat_size)
        send(
            parts.at[my_obs, my_lat],
            parts.at[my_obs, my_lat],
            sum_send.at[2],
            sum_recv.at[2],
            {"lat": peer},
        ).start()
        return carry

    lax.fori_loop(1, lat_size, spread_out, 0)

    send(
        bwd_out.at[:, pl.ds(0, group - 1)],
        bwd_in.at[pl.ds(0, group - 1)],
        bwd_send,
        bwd_recv,
        beside,
    ).wait_recv()
    landed(*stages[2]).wait_recv()

    def spread_wide(j, carry):
        send(
            parts.at[my_obs],
            parts.at[my_obs],
            sum_send.at[3],
            sum_recv.at[3],
            {"obs": lax.rem(my_obs + j, obs_size)},
        ).start()
        return carry

    lax.fori_loop(1, obs_size, spread_wide, 0)

    back = bwd_in[...].astype(F32).reshape(group * chunks, lat_dev, CHUNK, 2 * width)
    for part in range(2):
        lane = slice(part * width, (part + 1) * width)
        pre_ref[part * orders : (part + 1) * orders, :] = jnp.concatenate(
            [back[:, k, :, lane].reshape(orders, width) for k in range(lat_dev)], axis=1
        ).astype(BF16)

    def to_grid(i, carry):
        at = pl.multiple_of(i * tile, tile)
        got = dot(tab_t[pl.ds(at, tile), :], pre_ref[0 : 2 * orders, :]) * (1.0 / lon_count)
        for k in range(lat_dev):
            grid_out[k, pl.ds(at, tile), :] = (
                out_ref[k, pl.ds(at, tile), :] + got[:, k * width : (k + 1) * width]
            ).astype(BF16)
        return carry

    lax.fori_loop(0, lon_count // tile, to_grid, 0)

    landed(*stages[3]).wait_recv()
    for r in range(2):
        gain_out[r] = (
            parts[:, :, r * share : (r + 1) * share, :].astype(F32).reshape(degrees, width)
        )

    send(
        packed.at[pl.ds(0, group - 1)], obs_in.at[pl.ds(0, group - 1)], obs_send, obs_recv, beside
    ).wait_send()
    send(
        fwd_out.at[:, pl.ds(0, group - 1)],
        fwd_in.at[:, pl.ds(0, group - 1)],
        fwd_send,
        fwd_recv.at[0],
        beside,
    ).wait_send()
    send(
        bwd_out.at[:, pl.ds(0, group - 1)],
        bwd_in.at[pl.ds(0, group - 1)],
        bwd_send,
        bwd_recv,
        beside,
    ).wait_send()
    landed(*stages[0]).wait_send()
    landed(*stages[1]).wait_send()
    landed(*stages[2]).wait_send()
    landed(*stages[3]).wait_send()


def on_device(
    next_grad,
    pre_act,
    legendre,
    order_slots,
    quad_weights,
    spectral_gain,
    saved_coeffs,
    obs_value,
    obs_lat_frac,
    obs_lon_frac,
    obs_corner,
    obs_channel,
    slot_counts,
):
    lat_dev, lon_count, width = next_grad.shape
    lat_size = lax.axis_size("lat")
    obs_size = lax.axis_size("obs")
    group = lat_size * obs_size
    slot_dev, degrees, lat_count = legendre.shape
    orders = order_slots.shape[0]
    chunks = slot_dev // CHUNK
    rows = CHUNK * lat_dev
    lanes = 128
    side = lat_count * CHUNK
    joined = lanes // lat_count
    table = base_tables(orders, lon_count)
    table_t = np.ascontiguousarray(table.T)

    vmem = pl.BlockSpec(memory_space=pltpu.VMEM)
    anywhere = pl.BlockSpec(memory_space=pltpu.HBM)
    dma = pltpu.SemaphoreType.DMA
    share = degrees // group
    return pl.pallas_call(
        functools.partial(block_kernel, lat_size, obs_size),
        out_shape=(
            jax.ShapeDtypeStruct((lat_dev, lon_count, width), BF16),
            jax.ShapeDtypeStruct((2, degrees, width), F32),
        ),
        in_specs=[vmem] * 8 + [anywhere] * 7,
        out_specs=(vmem, vmem),
        scratch_shapes=[
            pltpu.VMEM((lat_dev, lon_count, width), BF16),
            pltpu.VMEM((lat_dev, lon_count, width), BF16),
            pltpu.VMEM((slot_dev, lat_count, degrees), BF16),
            pltpu.VMEM((2, degrees, width), F32),
            pltpu.VMEM((slot_dev, 2, degrees, width), BF16),
            pltpu.VMEM((orders, 2 * lon_count), BF16),
            pltpu.VMEM((2 * lon_count, orders), BF16),
            pltpu.VMEM((group, 8, lanes), F32),
            pltpu.VMEM((group, 8, lanes), F32),
            pltpu.VMEM((chunks, orders // chunks, orders), BF16),
            pltpu.VMEM((orders, orders), BF16),
            pltpu.VMEM((orders, lat_dev * 2 * width), BF16),
            pltpu.VMEM((lon_count, 2 * orders), BF16),
            pltpu.VMEM((slot_dev // joined, degrees, lanes), BF16),
            pltpu.VMEM((side, side), BF16),
            pltpu.VMEM((side, side), BF16),
            pltpu.VMEM((lat_dev, lon_count, width), F32),
            pltpu.VMEM((lat_dev, lon_count, width), F32),
            pltpu.VMEM((max(lon_count, 2 * orders), lat_dev * width), BF16),
            pltpu.VMEM((chunks, group, rows, 2 * width), BF16),
            pltpu.VMEM((chunks, group, rows, 2 * width), BF16),
            pltpu.VMEM((CHUNK, lanes, 2 * width), BF16),
            pltpu.VMEM((CHUNK, degrees, 2 * width), BF16),
            pltpu.VMEM((side, 2 * width), BF16),
            pltpu.VMEM((chunks, group, rows, 2 * width), BF16),
            pltpu.VMEM((group, chunks, rows, 2 * width), BF16),
            pltpu.VMEM((2, degrees, width), F32),
            pltpu.VMEM((obs_size, lat_size, 2 * share, width), BF16),
            pltpu.VMEM((obs_size, lat_size, 2 * share, width), BF16),
            pltpu.VMEM((lat_size, 2 * share, width), BF16),
            pltpu.VMEM((lat_size, 2 * share, width), BF16),
            pltpu.VMEM((obs_size, lat_size, 2 * share, width), BF16),
            dma((7,)),
            dma,
            dma,
            dma,
            dma((chunks,)),
            dma,
            dma,
            dma((4,)),
            dma((4,)),
        ],
        compiler_params=pltpu.CompilerParams(
            collective_id=0, has_side_effects=True, vmem_limit_bytes=44 * 1024 * 1024
        ),
        name="block_backward",
    )(
        obs_value,
        obs_lat_frac,
        obs_lon_frac,
        obs_corner,
        obs_channel,
        slot_counts,
        order_slots[None, :],
        quad_weights[None, :],
        next_grad,
        pre_act,
        jnp.transpose(legendre, (0, 2, 1)),
        spectral_gain,
        saved_coeffs,
        jnp.asarray(table),
        jnp.asarray(table_t),
    )


def kernel_fits(next_grad, legendre, obs_value, lat_size, obs_size):
    group = lat_size * obs_size
    lat_dev, lon_count, width = next_grad.shape
    slot_dev, degrees, lat_count = legendre.shape
    capacity = obs_value.shape[1]
    return (
        slot_dev % CHUNK == 0
        and (CHUNK * lat_dev) % 16 == 0
        and lat_count * CHUNK <= 512
        and 128 % lat_count == 0
        and CHUNK % (128 // lat_count) == 0
        and degrees % 128 == 0
        and lat_size > 1
        and obs_size > 1
        and width % 128 == 0
        and lon_count % 512 == 0
        and degrees % (16 * group) == 0
        and 128 % capacity == 0
        and group % (128 // capacity) == 0
    )


def device_path(*args):
    if kernel_fits(args[0], args[2], args[7], lax.axis_size("lat"), lax.axis_size("obs")):
        return on_device(*args)
    return plain_path(*args)


def solution(mesh):
    in_specs = (
        P(("lat", "obs"), None, "chan"),
        P(("lat", "obs"), None, "chan"),
        P(("lat", "obs"), None, None),
        P(),
        P(),
        P(None, None, "chan"),
        P(("lat", "obs"), None, None, "chan"),
        P(("lat", "obs"), None, None),
        P(("lat", "obs"), None, None),
        P(("lat", "obs"), None, None),
        P(("lat", "obs"), None, None),
        P(("lat", "obs"), None, None),
        P(("lat", "obs"), None),
    )
    out_specs = (P(("lat", "obs"), None, "chan"), P(None, None, "chan"))
    return jax.shard_map(
        device_path, mesh=mesh, in_specs=in_specs, out_specs=out_specs, check_vma=False
    )
```

```python
import functools
import math

import jax
import jax.numpy as jnp
import numpy as np
from jax import lax
from jax.experimental import pallas as pl
from jax.experimental.pallas import tpu as pltpu
from jax.sharding import PartitionSpec as P


def gelu_slope(pre_act):
    values = pre_act.astype(jnp.float32)
    normal_cdf = 0.5 * (1.0 + jax.scipy.special.erf(values * 0.7071067811865476))
    density = jnp.exp(-0.5 * values * values) * 0.3989422804014327
    return normal_cdf + values * density


def zonal_tables(orders, longitudes, lon_count, cos_weight, sin_weight):
    phase = orders[:, None] * longitudes[None, :] % lon_count
    angle = phase.astype(jnp.float32) * (2.0 * math.pi / lon_count)
    return (
        (cos_weight * jnp.cos(angle)).astype(jnp.bfloat16),
        (sin_weight * jnp.sin(angle)).astype(jnp.bfloat16),
    )


def adjoint_tiles(
    amounts, lat_frac, lon_frac, corners, channels, lat_dev, lon_count, chan_base, width
):
    received = amounts.size
    amounts = amounts.reshape(received)
    lat_frac = lat_frac.reshape(received)
    lon_frac = lon_frac.reshape(received)
    corners = corners.reshape(received)
    channels = channels.reshape(received)
    block_rows = min(512, received)
    cell_ids = lax.iota(jnp.int32, lat_dev * lon_count)
    chan_ids = chan_base + lax.iota(jnp.int32, width)
    nothing = jnp.zeros((), jnp.bfloat16)

    def add_block(counter, summed):
        offset = counter * block_rows
        lat_step = lax.dynamic_slice_in_dim(lat_frac, offset, block_rows).astype(jnp.float32)
        lon_step = lax.dynamic_slice_in_dim(lon_frac, offset, block_rows).astype(jnp.float32)
        corner_ids = lax.dynamic_slice_in_dim(corners, offset, block_rows)
        chan_rows = lax.dynamic_slice_in_dim(channels, offset, block_rows)
        amount_rows = lax.dynamic_slice_in_dim(amounts, offset, block_rows)
        top = corner_ids // lon_count
        left = corner_ids % lon_count
        right = (left + 1) % lon_count
        lower = top * lon_count
        upper = lower + lon_count
        weights = (
            (1.0 - lat_step) * (1.0 - lon_step),
            (1.0 - lat_step) * lon_step,
            lat_step * (1.0 - lon_step),
            lat_step * lon_step,
        )
        places = (lower + left, lower + right, upper + left, upper + right)
        stencil = jnp.zeros((block_rows, lat_dev * lon_count), jnp.bfloat16)
        for weight, place in zip(weights, places):
            stencil = stencil + jnp.where(
                cell_ids[None, :] == place[:, None], weight.astype(jnp.bfloat16)[:, None], nothing
            )
        sources = jnp.where(chan_rows[:, None] == chan_ids[None, :], amount_rows[:, None], nothing)
        return summed + lax.dot_general(
            stencil, sources, (((0,), (0,)), ((), ())), preferred_element_type=jnp.float32
        )

    start_sum = jnp.zeros((lat_dev * lon_count, width), jnp.float32)
    summed = lax.fori_loop(0, received // block_rows, add_block, start_sum)
    return summed.reshape(lat_dev, lon_count, width)


def plain_path(
    next_grad,
    pre_act,
    legendre,
    order_slots,
    quad_weights,
    spectral_gain,
    saved_coeffs,
    obs_value,
    obs_lat_frac,
    obs_lon_frac,
    obs_corner,
    obs_channel,
    slot_counts,
):
    lat_dev, lon_count, width = next_grad.shape
    lat_size = lax.axis_size("lat")
    obs_size = lax.axis_size("obs")
    slot_dev, degrees, lat_count = legendre.shape
    total_orders = order_slots.shape[0]
    capacity = obs_value.shape[1]
    alive_slots = lax.iota(jnp.int32, capacity)[:, None] < slot_counts[0][None, :]
    masked = jnp.where(alive_slots, obs_value[0], jnp.zeros((), jnp.bfloat16)).reshape(
        capacity, lat_size, obs_size
    )
    lat_frac = obs_lat_frac[0].reshape(capacity, lat_size, obs_size)
    lon_frac = obs_lon_frac[0].reshape(capacity, lat_size, obs_size)
    corners = obs_corner[0].reshape(capacity, lat_size, obs_size)
    channels = obs_channel[0].reshape(capacity, lat_size, obs_size)
    arrived = (
        lax.all_to_all(
            lax.all_to_all(masked, "lat", split_axis=1, concat_axis=1, tiled=True),
            "obs",
            split_axis=2,
            concat_axis=2,
            tiled=True,
        ),
        lax.all_to_all(
            lax.all_to_all(lat_frac, "lat", split_axis=1, concat_axis=1, tiled=True),
            "obs",
            split_axis=2,
            concat_axis=2,
            tiled=True,
        ),
        lax.all_to_all(
            lax.all_to_all(lon_frac, "lat", split_axis=1, concat_axis=1, tiled=True),
            "obs",
            split_axis=2,
            concat_axis=2,
            tiled=True,
        ),
        lax.all_to_all(
            lax.all_to_all(corners, "lat", split_axis=1, concat_axis=1, tiled=True),
            "obs",
            split_axis=2,
            concat_axis=2,
            tiled=True,
        ),
        lax.all_to_all(
            lax.all_to_all(channels, "lat", split_axis=1, concat_axis=1, tiled=True),
            "obs",
            split_axis=2,
            concat_axis=2,
            tiled=True,
        ),
    )
    chan_base = lax.axis_index("chan") * width
    obs_grad = adjoint_tiles(
        arrived[0],
        arrived[1],
        arrived[2],
        arrived[3],
        arrived[4],
        lat_dev,
        lon_count,
        chan_base,
        width,
    )
    out_grad = next_grad.astype(jnp.float32) + obs_grad
    pre_grad = (out_grad * gelu_slope(pre_act)).astype(jnp.bfloat16)
    longitudes = lax.iota(jnp.int32, lon_count)
    crossed_orders = jnp.transpose(
        order_slots.reshape(lat_size, obs_size, slot_dev), (1, 0, 2)
    ).reshape(total_orders)
    legendre_view = legendre.reshape(slot_dev, degrees, lat_size, obs_size, lat_dev)
    weight_view = quad_weights.reshape(lat_size, obs_size, lat_dev)
    factor = jnp.where(order_slots == 0, 1.0, 2.0).astype(jnp.float32)[:, None]
    cosine, sine = zonal_tables(order_slots, longitudes, lon_count, factor, -factor)
    real_part = jnp.einsum("mn,knc->mkc", cosine, pre_grad, preferred_element_type=jnp.float32)
    imag_part = jnp.einsum("mn,knc->mkc", sine, pre_grad, preferred_element_type=jnp.float32)
    by_order = lax.all_to_all(
        lax.all_to_all(
            jnp.stack([real_part, imag_part], axis=1).astype(jnp.bfloat16),
            "lat",
            split_axis=0,
            concat_axis=2,
            tiled=True,
        ),
        "obs",
        split_axis=0,
        concat_axis=2,
        tiled=True,
    )
    order_view = by_order.reshape(slot_dev, 2, obs_size, lat_size, lat_dev, width)
    up_grad = jnp.einsum(
        "iljka,irkjac->irlc", legendre_view, order_view, preferred_element_type=jnp.float32
    )
    saved = saved_coeffs.astype(jnp.float32)
    gain_terms = jnp.stack(
        [
            jnp.sum(up_grad[:, 0] * saved[:, 0] + up_grad[:, 1] * saved[:, 1], axis=0),
            jnp.sum(up_grad[:, 1] * saved[:, 0] - up_grad[:, 0] * saved[:, 1], axis=0),
        ]
    )
    gain_grad = lax.psum(gain_terms, ("lat", "obs"))
    gain_real = spectral_gain[0]
    gain_imag = spectral_gain[1]
    coeff_grad = jnp.stack(
        [
            gain_real * up_grad[:, 0] + gain_imag * up_grad[:, 1],
            gain_real * up_grad[:, 1] - gain_imag * up_grad[:, 0],
        ],
        axis=1,
    ).astype(jnp.bfloat16)
    analysed = jnp.einsum(
        "iljka,irlc->irjkac", legendre_view, coeff_grad, preferred_element_type=jnp.float32
    )
    lat_grad = (
        (analysed * weight_view[None, None, :, :, :, None])
        .astype(jnp.bfloat16)
        .reshape(slot_dev, 2, lat_count, width)
    )
    by_lat = lax.all_to_all(
        lax.all_to_all(lat_grad, "lat", split_axis=2, concat_axis=0, tiled=True),
        "obs",
        split_axis=2,
        concat_axis=0,
        tiled=True,
    )
    scale = jnp.full((total_orders, 1), 1.0 / lon_count, jnp.float32)
    cosine, sine = zonal_tables(crossed_orders, longitudes, lon_count, scale, -scale)
    spectral_grad = jnp.einsum(
        "mkc,mn->knc", by_lat[:, 0], cosine, preferred_element_type=jnp.float32
    )
    spectral_grad = spectral_grad + jnp.einsum(
        "mkc,mn->knc", by_lat[:, 1], sine, preferred_element_type=jnp.float32
    )
    grid_grad = (out_grad + spectral_grad).astype(jnp.bfloat16)
    return (grid_grad, gain_grad)


CHUNK = 8
F32 = jnp.float32
BF16 = jnp.bfloat16
MESH = pl.DeviceIdType.MESH


def base_tables(order_count, lon_count):
    phase = np.arange(order_count)[:, None] * np.arange(lon_count)[None, :] % lon_count
    angle = phase.astype(np.float32) * np.float32(2.0 * math.pi / lon_count)
    return np.concatenate([np.cos(angle), -np.sin(angle)], axis=1).astype(jnp.bfloat16)


def dot(a, b):
    return jnp.dot(a, b, preferred_element_type=F32)


def block_kernel(
    lat_size,
    obs_size,
    value_ref,
    lat_frac_ref,
    lon_frac_ref,
    corner_ref,
    channel_ref,
    count_ref,
    order_row,
    quad_row,
    next_hbm,
    act_hbm,
    leg_hbm,
    gain_hbm,
    saved_hbm,
    table_hbm,
    table_t_hbm,
    grid_out,
    gain_out,
    next_ref,
    act_ref,
    leg_ref,
    gain_ref,
    saved_ref,
    table_ref,
    table_t_ref,
    packed,
    obs_in,
    hot,
    hot_t,
    waves,
    tab_t,
    leg_t,
    to_slot,
    to_lat,
    slope_ref,
    out_ref,
    pre_ref,
    fwd_out,
    fwd_in,
    by_slot,
    coeff_ref,
    by_lat,
    bwd_out,
    bwd_in,
    grid_ref,
    total,
    near_out,
    near_in,
    far_out,
    far_in,
    parts,
    local_sem,
    obs_send,
    obs_recv,
    fwd_send,
    fwd_recv,
    bwd_send,
    bwd_recv,
    sum_send,
    sum_recv,
    leave_sem,
):
    group = lat_size * obs_size
    my_lat = lax.axis_index("lat")
    my_obs = lax.axis_index("obs")
    me = my_lat * obs_size + my_obs
    lat_dev, lon_count, width = next_ref.shape
    slot_dev, lat_count, degrees = leg_ref.shape
    orders = order_row.shape[1]
    capacity = value_ref.shape[1]
    chunks = slot_dev // CHUNK
    rows = CHUNK * lat_dev
    lanes = packed.shape[2]
    tile = 256

    others = []
    for j in range(1, group):
        lat_at = lax.rem(my_lat + j // obs_size, lat_size)
        obs_at = lax.rem(my_obs + j % obs_size, obs_size)
        others.append((lat_at * obs_size + obs_at, {"lat": lat_at, "obs": obs_at}))

    def peers(body):
        for peer, where in others:
            body(peer, where)

    def send(src, dst, send_sem, recv_sem, target):
        return pltpu.make_async_remote_copy(
            src_ref=src,
            dst_ref=dst,
            send_sem=send_sem,
            recv_sem=recv_sem,
            device_id=target,
            device_id_type=MESH,
        )

    beside = {"obs": lax.rem(my_obs + 1, obs_size)}

    def iota(shape, axis):
        return lax.broadcasted_iota(jnp.int32, shape, axis)

    def column(row):
        side = row.shape[1]
        same = iota((side, side), 0) == iota((side, side), 1)
        return jnp.sum(jnp.where(same, row, 0.0), axis=1, keepdims=True)

    barrier = pltpu.get_barrier_semaphore()
    peers(
        lambda _, where: pl.semaphore_signal(
            barrier, inc=1, device_id=where, device_id_type=MESH
        )
    )
    local = [
        pltpu.make_async_copy(src, dst, local_sem.at[i])
        for i, (src, dst) in enumerate(
            (
                (act_hbm, act_ref),
                (table_hbm, table_ref),
                (next_hbm, next_ref),
                (table_t_hbm, table_t_ref),
                (leg_hbm, leg_ref),
                (gain_hbm, gain_ref),
                (saved_hbm, saved_ref),
            )
        )
    ]
    for copy in local[:3]:
        copy.start()

    alive = iota((capacity, group), 0) < count_ref[...]
    lat_step = lat_frac_ref[0].astype(F32)
    lon_step = lon_frac_ref[0].astype(F32)
    corner = corner_ref[0]
    fields = (
        jnp.where(alive, value_ref[0].astype(F32), 0.0),
        (1.0 - lat_step) * (1.0 - lon_step),
        (1.0 - lat_step) * lon_step,
        lat_step * (1.0 - lon_step),
        lat_step * lon_step,
        (corner // 128).astype(F32),
        (corner % 128).astype(F32),
        channel_ref[0].astype(F32),
    )
    at_row = iota((8 * group, group), 0)
    at_tile = iota((8 * group, group), 1)
    by_row = jnp.zeros((8 * group, capacity), F32)
    for i, field in enumerate(fields):
        pick = jnp.where(at_row == at_tile * 8 + i, 1.0, 0.0).astype(BF16)
        by_row = by_row + lax.dot_general(
            pick, field.astype(BF16), (((1,), (1,)), ((), ())), preferred_element_type=F32
        )
    spots = lanes // capacity
    spread = jnp.where(
        iota((capacity, lanes), 1) == lax.rem(me, spots) * capacity + iota((capacity, lanes), 0),
        1.0,
        0.0,
    ).astype(BF16)
    packed[...] = dot(by_row.astype(BF16), spread).reshape(group, 8, lanes)
    obs_in[me] = packed[me]

    order_f = order_row[...].astype(F32)
    order_col = column(order_f).reshape(group, chunks, CHUNK, 1)
    per = orders // chunks
    for q in range(chunks):
        here = order_col[:, q].reshape(per, 1)
        hot[q] = jnp.where(iota((per, orders), 1).astype(F32) == here, 1.0, 0.0).astype(BF16)

    pl.semaphore_wait(barrier, group - 1)
    peers(
        lambda peer, where: send(
            packed.at[peer], obs_in.at[me], obs_send, obs_recv, where
        ).start()
    )
    for copy in local[3:]:
        copy.start()

    local[0].wait()
    for k in range(lat_dev):
        values = act_ref[k].astype(F32)
        cdf = 0.5 * (1.0 + lax.erf(values * 0.7071067811865476))
        density = jnp.exp(-0.5 * values * values) * 0.3989422804014327
        slope_ref[k] = cdf + values * density
    local[2].wait()
    send(
        packed.at[pl.ds(0, group - 1)],
        obs_in.at[pl.ds(0, group - 1)],
        obs_send,
        obs_recv,
        beside,
    ).wait_recv()
    halves = []
    for h in range(group // spots):
        halves.append(jnp.sum(obs_in[h * spots : (h + 1) * spots], axis=0))
    seen = jnp.concatenate(halves, axis=1)
    received = seen.shape[1]
    corner = seen[5:6].astype(jnp.int32) * 128 + seen[6:7].astype(jnp.int32)
    channel = seen[7:8].astype(jnp.int32)
    left = corner % lon_count
    right = corner - left + (left + 1) % lon_count
    places = (corner, right, corner + lon_count, right + lon_count)
    chan_ids = lax.axis_index("chan") * width + iota((width, received), 0)
    amounts = jnp.where(chan_ids == channel, seen[0:1], 0.0).astype(BF16)
    for k in range(lat_dev):
        for half in range(2):
            span = lon_count // 2
            begin = half * span
            cells = k * lon_count + begin + iota((span, received), 0)
            stencil = jnp.zeros((span, received), F32)
            for w, at in enumerate(places):
                stencil = jnp.where(cells == at, seen[1 + w : 2 + w], stencil)
            added = lax.dot_general(
                stencil.astype(BF16), amounts, (((1,), (1,)), ((), ())), preferred_element_type=F32
            )
            here = slice(begin, begin + span)
            out_grad = next_ref[k, here].astype(F32) + added
            out_ref[k, here] = out_grad
            pre_ref[here, k * width : (k + 1) * width] = (out_grad * slope_ref[k, here]).astype(BF16)

    local[1].wait()
    factor = jnp.where(iota((orders, 1), 0) == 0, 1.0, 2.0)
    for part in range(2):
        got = dot(table_ref[:, part * lon_count : (part + 1) * lon_count], pre_ref[...])
        for k in range(lat_dev):
            begin = (k * 2 + part) * width
            waves[:, begin : begin + width] = (
                got[:, k * width : (k + 1) * width] * factor
            ).astype(BF16)

    def zonal(q, carry):
        got = dot(hot[q], waves[...]).reshape(group, CHUNK, lat_dev * 2 * width)
        fwd_out[q] = jnp.concatenate(
            [got[:, :, k * 2 * width : (k + 1) * 2 * width] for k in range(lat_dev)], axis=1
        ).astype(BF16)
        fwd_in[q, me] = fwd_out[q, me]
        peers(
            lambda peer, where: send(
                fwd_out.at[q, peer], fwd_in.at[q, me], fwd_send, fwd_recv.at[q], where
            ).start()
        )
        return carry

    lax.fori_loop(0, chunks, zonal, 0)

    side = lat_count * CHUNK
    first = iota((side, side), 0)
    second = iota((side, side), 1)
    to_lat[...] = jnp.where(
        (first // CHUNK == second % lat_count) & (first % CHUNK == second // lat_count), 1.0, 0.0
    ).astype(BF16)
    to_slot[...] = jnp.where(
        (second // CHUNK == first % lat_count) & (second % CHUNK == first // lat_count), 1.0, 0.0
    ).astype(BF16)
    joined = lanes // lat_count
    for copy in local[4:]:
        copy.wait()

    def turn(j, carry):
        table = leg_ref[pl.ds(j * joined, joined)].reshape(lanes, degrees)
        leg_t[j] = table.T
        return carry

    lax.fori_loop(0, slot_dev // joined, turn, 0)
    total[...] = jnp.zeros_like(total)
    quad = column(quad_row[...])

    def make_tab_t(part):
        def step(i, carry):
            at = pl.multiple_of(i * tile, tile)
            got = dot(table_t_ref[pl.ds(part * lon_count + at, tile), :], hot_t[...])
            tab_t[pl.ds(at, tile), part * orders : (part + 1) * orders] = got.astype(BF16)
            return carry

        lax.fori_loop(0, lon_count // tile, step, 0)

    share = degrees // group

    def around(axis, size, mine, src, dst, sem):
        def step(j, carry):
            peer = lax.rem(mine + j, size)
            send(
                src.at[peer],
                dst.at[mine],
                sum_send.at[sem],
                sum_recv.at[sem],
                {axis: peer},
            ).start()
            return carry

        lax.fori_loop(1, size, step, 0)

    def landed(axis, size, mine, src, dst, sem):
        return send(
            src.at[pl.ds(0, size - 1)],
            dst.at[pl.ds(0, size - 1)],
            sum_send.at[sem],
            sum_recv.at[sem],
            {axis: lax.rem(mine + 1, size)},
        )

    stages = (
        ("obs", obs_size, my_obs, near_out, near_in, 0),
        ("lat", lat_size, my_lat, far_out, far_in, 1),
        ("lat", lat_size, my_lat, far_out, far_in, 2),
        ("obs", obs_size, my_obs, parts, parts, 3),
    )
    def start_sum():
        for r in range(2):
            near_out[:, :, r * share : (r + 1) * share, :] = (
                total[r].reshape(obs_size, lat_size, share, width).astype(BF16)
            )
        near_in[my_obs] = near_out[my_obs]
        around(*stages[0])

    span = 128

    def degrees_of(q, carry):
        send(
            fwd_out.at[q, pl.ds(0, group - 1)],
            fwd_in.at[q, pl.ds(0, group - 1)],
            fwd_send,
            fwd_recv.at[q],
            beside,
        ).wait_recv()
        arrived = dot(to_slot[...], fwd_in[q].reshape(side, 2 * width)).astype(BF16)
        owner = iota((lanes, 2 * width), 0) // lat_count
        for i in range(CHUNK):
            begin = i // joined * lanes
            by_slot[i] = jnp.where(
                owner == i % joined, arrived[begin : begin + lanes].astype(F32), 0.0
            ).astype(BF16)

        def degree_tile(t, inner):
            here = pl.ds(pl.multiple_of(t * span, span), span)
            gain_real = gain_ref[0, here, :]
            gain_imag = gain_ref[1, here, :]
            sum_real = total[0, here, :]
            sum_imag = total[1, here, :]
            for i in range(CHUNK):
                s = q * CHUNK + i
                up = dot(leg_t[q * (CHUNK // joined) + i // joined, here, :], by_slot[i])
                up_real = up[:, :width]
                up_imag = up[:, width:]
                saved_real = saved_ref[s, 0, here, :].astype(F32)
                saved_imag = saved_ref[s, 1, here, :].astype(F32)
                sum_real = sum_real + (up_real * saved_real + up_imag * saved_imag)
                sum_imag = sum_imag + (up_imag * saved_real - up_real * saved_imag)
                coeff_ref[i, here, :width] = (
                    gain_real * up_real + gain_imag * up_imag
                ).astype(BF16)
                coeff_ref[i, here, width:] = (
                    gain_real * up_imag - gain_imag * up_real
                ).astype(BF16)
            total[0, here, :] = sum_real
            total[1, here, :] = sum_imag
            return inner

        lax.fori_loop(0, degrees // span, degree_tile, 0)
        pl.when(q == chunks - 1)(start_sum)
        for i in range(CHUNK):
            by_lat[i * lat_count : (i + 1) * lat_count, :] = (
                dot(leg_ref[q * CHUNK + i], coeff_ref[i]) * quad
            ).astype(BF16)
        bwd_out[q] = dot(to_lat[...], by_lat[...]).astype(BF16).reshape(group, rows, 2 * width)
        bwd_in[me, q] = bwd_out[q, me]
        peers(
            lambda peer, where: send(
                bwd_out.at[q, peer], bwd_in.at[me, q], bwd_send, bwd_recv, where
            ).start()
        )
        return carry

    lax.fori_loop(0, chunks, degrees_of, 0)

    hot_t[...] = jnp.where(iota((orders, orders), 0) == order_row[...], 1.0, 0.0).astype(BF16)
    local[3].wait()
    make_tab_t(0)
    landed(*stages[0]).wait_recv()
    far_out[...] = jnp.sum(near_in[...].astype(F32), axis=0).astype(BF16)
    far_in[my_lat] = far_out[my_lat]
    around(*stages[1])
    make_tab_t(1)
    landed(*stages[1]).wait_recv()
    parts[my_obs, my_lat] = jnp.sum(far_in[...].astype(F32), axis=0).astype(BF16)

    def spread_out(j, carry):
        peer = lax.rem(my_lat + j, lat_size)
        send(
            parts.at[my_obs, my_lat],
            parts.at[my_obs, my_lat],
            sum_send.at[2],
            sum_recv.at[2],
            {"lat": peer},
        ).start()
        return carry

    lax.fori_loop(1, lat_size, spread_out, 0)

    landed(*stages[2]).wait_recv()

    def spread_wide(j, carry):
        send(
            parts.at[my_obs],
            parts.at[my_obs],
            sum_send.at[3],
            sum_recv.at[3],
            {"obs": lax.rem(my_obs + j, obs_size)},
        ).start()
        return carry

    lax.fori_loop(1, obs_size, spread_wide, 0)

    send(
        bwd_out.at[:, pl.ds(0, group - 1)],
        bwd_in.at[pl.ds(0, group - 1)],
        bwd_send,
        bwd_recv,
        beside,
    ).wait_recv()

    back = bwd_in[...].astype(F32).reshape(group * chunks, lat_dev, CHUNK, 2 * width)
    for part in range(2):
        lane = slice(part * width, (part + 1) * width)
        pre_ref[part * orders : (part + 1) * orders, :] = jnp.concatenate(
            [back[:, k, :, lane].reshape(orders, width) for k in range(lat_dev)], axis=1
        ).astype(BF16)

    leaving = []
    for i in range(lon_count // tile):
        here = slice(i * tile, (i + 1) * tile)
        got = dot(tab_t[here, :], pre_ref[0 : 2 * orders, :]) * (1.0 / lon_count)
        for k in range(lat_dev):
            grid_ref[k, here, :] = (
                out_ref[k, here, :] + got[:, k * width : (k + 1) * width]
            ).astype(BF16)
        leaving.append(
            pltpu.make_async_copy(grid_ref.at[:, here], grid_out.at[:, here], leave_sem.at[i])
        )
        leaving[-1].start()

    landed(*stages[3]).wait_recv()
    for r in range(2):
        leaving.append(
            pltpu.make_async_copy(
                parts.at[:, :, r * share : (r + 1) * share],
                gain_out.at[r],
                leave_sem.at[lon_count // tile + r],
            )
        )
        leaving[-1].start()

    send(
        packed.at[pl.ds(0, group - 1)], obs_in.at[pl.ds(0, group - 1)], obs_send, obs_recv, beside
    ).wait_send()
    send(
        fwd_out.at[:, pl.ds(0, group - 1)],
        fwd_in.at[:, pl.ds(0, group - 1)],
        fwd_send,
        fwd_recv.at[0],
        beside,
    ).wait_send()
    send(
        bwd_out.at[:, pl.ds(0, group - 1)],
        bwd_in.at[pl.ds(0, group - 1)],
        bwd_send,
        bwd_recv,
        beside,
    ).wait_send()
    landed(*stages[0]).wait_send()
    landed(*stages[1]).wait_send()
    landed(*stages[2]).wait_send()
    landed(*stages[3]).wait_send()
    for copy in leaving:
        copy.wait()


def on_device(
    next_grad,
    pre_act,
    legendre,
    order_slots,
    quad_weights,
    spectral_gain,
    saved_coeffs,
    obs_value,
    obs_lat_frac,
    obs_lon_frac,
    obs_corner,
    obs_channel,
    slot_counts,
):
    lat_dev, lon_count, width = next_grad.shape
    lat_size = lax.axis_size("lat")
    obs_size = lax.axis_size("obs")
    group = lat_size * obs_size
    slot_dev, degrees, lat_count = legendre.shape
    orders = order_slots.shape[0]
    chunks = slot_dev // CHUNK
    rows = CHUNK * lat_dev
    lanes = 128
    side = lat_count * CHUNK
    joined = lanes // lat_count
    table = base_tables(orders, lon_count)
    table_t = np.ascontiguousarray(table.T)

    vmem = pl.BlockSpec(memory_space=pltpu.VMEM)
    anywhere = pl.BlockSpec(memory_space=pltpu.HBM)
    dma = pltpu.SemaphoreType.DMA
    share = degrees // group
    grid_grad, gain_parts = pl.pallas_call(
        functools.partial(block_kernel, lat_size, obs_size),
        out_shape=(
            jax.ShapeDtypeStruct((lat_dev, lon_count, width), BF16),
            jax.ShapeDtypeStruct((2, obs_size, lat_size, share, width), BF16),
        ),
        in_specs=[vmem] * 8 + [anywhere] * 7,
        out_specs=(pl.BlockSpec(memory_space=pl.ANY), pl.BlockSpec(memory_space=pl.ANY)),
        scratch_shapes=[
            pltpu.VMEM((lat_dev, lon_count, width), BF16),
            pltpu.VMEM((lat_dev, lon_count, width), BF16),
            pltpu.VMEM((slot_dev, lat_count, degrees), BF16),
            pltpu.VMEM((2, degrees, width), F32),
            pltpu.VMEM((slot_dev, 2, degrees, width), BF16),
            pltpu.VMEM((orders, 2 * lon_count), BF16),
            pltpu.VMEM((2 * lon_count, orders), BF16),
            pltpu.VMEM((group, 8, lanes), F32),
            pltpu.VMEM((group, 8, lanes), F32),
            pltpu.VMEM((chunks, orders // chunks, orders), BF16),
            pltpu.VMEM((orders, orders), BF16),
            pltpu.VMEM((orders, lat_dev * 2 * width), BF16),
            pltpu.VMEM((lon_count, 2 * orders), BF16),
            pltpu.VMEM((slot_dev // joined, degrees, lanes), BF16),
            pltpu.VMEM((side, side), BF16),
            pltpu.VMEM((side, side), BF16),
            pltpu.VMEM((lat_dev, lon_count, width), F32),
            pltpu.VMEM((lat_dev, lon_count, width), F32),
            pltpu.VMEM((max(lon_count, 2 * orders), lat_dev * width), BF16),
            pltpu.VMEM((chunks, group, rows, 2 * width), BF16),
            pltpu.VMEM((chunks, group, rows, 2 * width), BF16),
            pltpu.VMEM((CHUNK, lanes, 2 * width), BF16),
            pltpu.VMEM((CHUNK, degrees, 2 * width), BF16),
            pltpu.VMEM((side, 2 * width), BF16),
            pltpu.VMEM((chunks, group, rows, 2 * width), BF16),
            pltpu.VMEM((group, chunks, rows, 2 * width), BF16),
            pltpu.VMEM((lat_dev, lon_count, width), BF16),
            pltpu.VMEM((2, degrees, width), F32),
            pltpu.VMEM((obs_size, lat_size, 2 * share, width), BF16),
            pltpu.VMEM((obs_size, lat_size, 2 * share, width), BF16),
            pltpu.VMEM((lat_size, 2 * share, width), BF16),
            pltpu.VMEM((lat_size, 2 * share, width), BF16),
            pltpu.VMEM((obs_size, lat_size, 2 * share, width), BF16),
            dma((7,)),
            dma,
            dma,
            dma,
            dma((chunks,)),
            dma,
            dma,
            dma((4,)),
            dma((4,)),
            dma((lon_count // 256 + 2,)),
        ],
        compiler_params=pltpu.CompilerParams(
            collective_id=0, has_side_effects=True, vmem_limit_bytes=60 * 1024 * 1024
        ),
        name="block_backward",
    )(
        obs_value,
        obs_lat_frac,
        obs_lon_frac,
        obs_corner,
        obs_channel,
        slot_counts,
        order_slots[None, :],
        quad_weights[None, :],
        next_grad,
        pre_act,
        jnp.transpose(legendre, (0, 2, 1)),
        spectral_gain,
        saved_coeffs,
        jnp.asarray(table),
        jnp.asarray(table_t),
    )
    return grid_grad, gain_parts.astype(F32).reshape(2, degrees, width)


def kernel_fits(next_grad, legendre, obs_value, lat_size, obs_size):
    group = lat_size * obs_size
    lat_dev, lon_count, width = next_grad.shape
    slot_dev, degrees, lat_count = legendre.shape
    capacity = obs_value.shape[1]
    return (
        slot_dev % CHUNK == 0
        and (CHUNK * lat_dev) % 16 == 0
        and lat_count * CHUNK <= 512
        and 128 % lat_count == 0
        and CHUNK % (128 // lat_count) == 0
        and degrees % 128 == 0
        and lat_size > 1
        and obs_size > 1
        and width % 128 == 0
        and lon_count % 512 == 0
        and degrees % (16 * group) == 0
        and 128 % capacity == 0
        and group % (128 // capacity) == 0
    )


def device_path(*args):
    if kernel_fits(args[0], args[2], args[7], lax.axis_size("lat"), lax.axis_size("obs")):
        return on_device(*args)
    return plain_path(*args)


def solution(mesh):
    in_specs = (
        P(("lat", "obs"), None, "chan"),
        P(("lat", "obs"), None, "chan"),
        P(("lat", "obs"), None, None),
        P(),
        P(),
        P(None, None, "chan"),
        P(("lat", "obs"), None, None, "chan"),
        P(("lat", "obs"), None, None),
        P(("lat", "obs"), None, None),
        P(("lat", "obs"), None, None),
        P(("lat", "obs"), None, None),
        P(("lat", "obs"), None, None),
        P(("lat", "obs"), None),
    )
    out_specs = (P(("lat", "obs"), None, "chan"), P(None, None, "chan"))
    return jax.shard_map(
        device_path, mesh=mesh, in_specs=in_specs, out_specs=out_specs, check_vma=False
    )
```

```python
import functools
import math

import jax
import jax.numpy as jnp
import numpy as np
from jax import lax
from jax.experimental import pallas as pl
from jax.experimental.pallas import tpu as pltpu
from jax.sharding import PartitionSpec as P


def gelu_slope(pre_act):
    values = pre_act.astype(jnp.float32)
    normal_cdf = 0.5 * (1.0 + jax.scipy.special.erf(values * 0.7071067811865476))
    density = jnp.exp(-0.5 * values * values) * 0.3989422804014327
    return normal_cdf + values * density


def zonal_tables(orders, longitudes, lon_count, cos_weight, sin_weight):
    phase = orders[:, None] * longitudes[None, :] % lon_count
    angle = phase.astype(jnp.float32) * (2.0 * math.pi / lon_count)
    return (
        (cos_weight * jnp.cos(angle)).astype(jnp.bfloat16),
        (sin_weight * jnp.sin(angle)).astype(jnp.bfloat16),
    )


def adjoint_tiles(
    amounts, lat_frac, lon_frac, corners, channels, lat_dev, lon_count, chan_base, width
):
    received = amounts.size
    amounts = amounts.reshape(received)
    lat_frac = lat_frac.reshape(received)
    lon_frac = lon_frac.reshape(received)
    corners = corners.reshape(received)
    channels = channels.reshape(received)
    block_rows = min(512, received)
    cell_ids = lax.iota(jnp.int32, lat_dev * lon_count)
    chan_ids = chan_base + lax.iota(jnp.int32, width)
    nothing = jnp.zeros((), jnp.bfloat16)

    def add_block(counter, summed):
        offset = counter * block_rows
        lat_step = lax.dynamic_slice_in_dim(lat_frac, offset, block_rows).astype(jnp.float32)
        lon_step = lax.dynamic_slice_in_dim(lon_frac, offset, block_rows).astype(jnp.float32)
        corner_ids = lax.dynamic_slice_in_dim(corners, offset, block_rows)
        chan_rows = lax.dynamic_slice_in_dim(channels, offset, block_rows)
        amount_rows = lax.dynamic_slice_in_dim(amounts, offset, block_rows)
        top = corner_ids // lon_count
        left = corner_ids % lon_count
        right = (left + 1) % lon_count
        lower = top * lon_count
        upper = lower + lon_count
        weights = (
            (1.0 - lat_step) * (1.0 - lon_step),
            (1.0 - lat_step) * lon_step,
            lat_step * (1.0 - lon_step),
            lat_step * lon_step,
        )
        places = (lower + left, lower + right, upper + left, upper + right)
        stencil = jnp.zeros((block_rows, lat_dev * lon_count), jnp.bfloat16)
        for weight, place in zip(weights, places):
            stencil = stencil + jnp.where(
                cell_ids[None, :] == place[:, None], weight.astype(jnp.bfloat16)[:, None], nothing
            )
        sources = jnp.where(chan_rows[:, None] == chan_ids[None, :], amount_rows[:, None], nothing)
        return summed + lax.dot_general(
            stencil, sources, (((0,), (0,)), ((), ())), preferred_element_type=jnp.float32
        )

    start_sum = jnp.zeros((lat_dev * lon_count, width), jnp.float32)
    summed = lax.fori_loop(0, received // block_rows, add_block, start_sum)
    return summed.reshape(lat_dev, lon_count, width)


def plain_path(
    next_grad,
    pre_act,
    legendre,
    order_slots,
    quad_weights,
    spectral_gain,
    saved_coeffs,
    obs_value,
    obs_lat_frac,
    obs_lon_frac,
    obs_corner,
    obs_channel,
    slot_counts,
):
    lat_dev, lon_count, width = next_grad.shape
    lat_size = lax.axis_size("lat")
    obs_size = lax.axis_size("obs")
    slot_dev, degrees, lat_count = legendre.shape
    total_orders = order_slots.shape[0]
    capacity = obs_value.shape[1]
    alive_slots = lax.iota(jnp.int32, capacity)[:, None] < slot_counts[0][None, :]
    masked = jnp.where(alive_slots, obs_value[0], jnp.zeros((), jnp.bfloat16)).reshape(
        capacity, lat_size, obs_size
    )
    lat_frac = obs_lat_frac[0].reshape(capacity, lat_size, obs_size)
    lon_frac = obs_lon_frac[0].reshape(capacity, lat_size, obs_size)
    corners = obs_corner[0].reshape(capacity, lat_size, obs_size)
    channels = obs_channel[0].reshape(capacity, lat_size, obs_size)
    arrived = (
        lax.all_to_all(
            lax.all_to_all(masked, "lat", split_axis=1, concat_axis=1, tiled=True),
            "obs",
            split_axis=2,
            concat_axis=2,
            tiled=True,
        ),
        lax.all_to_all(
            lax.all_to_all(lat_frac, "lat", split_axis=1, concat_axis=1, tiled=True),
            "obs",
            split_axis=2,
            concat_axis=2,
            tiled=True,
        ),
        lax.all_to_all(
            lax.all_to_all(lon_frac, "lat", split_axis=1, concat_axis=1, tiled=True),
            "obs",
            split_axis=2,
            concat_axis=2,
            tiled=True,
        ),
        lax.all_to_all(
            lax.all_to_all(corners, "lat", split_axis=1, concat_axis=1, tiled=True),
            "obs",
            split_axis=2,
            concat_axis=2,
            tiled=True,
        ),
        lax.all_to_all(
            lax.all_to_all(channels, "lat", split_axis=1, concat_axis=1, tiled=True),
            "obs",
            split_axis=2,
            concat_axis=2,
            tiled=True,
        ),
    )
    chan_base = lax.axis_index("chan") * width
    obs_grad = adjoint_tiles(
        arrived[0],
        arrived[1],
        arrived[2],
        arrived[3],
        arrived[4],
        lat_dev,
        lon_count,
        chan_base,
        width,
    )
    out_grad = next_grad.astype(jnp.float32) + obs_grad
    pre_grad = (out_grad * gelu_slope(pre_act)).astype(jnp.bfloat16)
    longitudes = lax.iota(jnp.int32, lon_count)
    crossed_orders = jnp.transpose(
        order_slots.reshape(lat_size, obs_size, slot_dev), (1, 0, 2)
    ).reshape(total_orders)
    legendre_view = legendre.reshape(slot_dev, degrees, lat_size, obs_size, lat_dev)
    weight_view = quad_weights.reshape(lat_size, obs_size, lat_dev)
    factor = jnp.where(order_slots == 0, 1.0, 2.0).astype(jnp.float32)[:, None]
    cosine, sine = zonal_tables(order_slots, longitudes, lon_count, factor, -factor)
    real_part = jnp.einsum("mn,knc->mkc", cosine, pre_grad, preferred_element_type=jnp.float32)
    imag_part = jnp.einsum("mn,knc->mkc", sine, pre_grad, preferred_element_type=jnp.float32)
    by_order = lax.all_to_all(
        lax.all_to_all(
            jnp.stack([real_part, imag_part], axis=1).astype(jnp.bfloat16),
            "lat",
            split_axis=0,
            concat_axis=2,
            tiled=True,
        ),
        "obs",
        split_axis=0,
        concat_axis=2,
        tiled=True,
    )
    order_view = by_order.reshape(slot_dev, 2, obs_size, lat_size, lat_dev, width)
    up_grad = jnp.einsum(
        "iljka,irkjac->irlc", legendre_view, order_view, preferred_element_type=jnp.float32
    )
    saved = saved_coeffs.astype(jnp.float32)
    gain_terms = jnp.stack(
        [
            jnp.sum(up_grad[:, 0] * saved[:, 0] + up_grad[:, 1] * saved[:, 1], axis=0),
            jnp.sum(up_grad[:, 1] * saved[:, 0] - up_grad[:, 0] * saved[:, 1], axis=0),
        ]
    )
    gain_grad = lax.psum(gain_terms, ("lat", "obs"))
    gain_real = spectral_gain[0]
    gain_imag = spectral_gain[1]
    coeff_grad = jnp.stack(
        [
            gain_real * up_grad[:, 0] + gain_imag * up_grad[:, 1],
            gain_real * up_grad[:, 1] - gain_imag * up_grad[:, 0],
        ],
        axis=1,
    ).astype(jnp.bfloat16)
    analysed = jnp.einsum(
        "iljka,irlc->irjkac", legendre_view, coeff_grad, preferred_element_type=jnp.float32
    )
    lat_grad = (
        (analysed * weight_view[None, None, :, :, :, None])
        .astype(jnp.bfloat16)
        .reshape(slot_dev, 2, lat_count, width)
    )
    by_lat = lax.all_to_all(
        lax.all_to_all(lat_grad, "lat", split_axis=2, concat_axis=0, tiled=True),
        "obs",
        split_axis=2,
        concat_axis=0,
        tiled=True,
    )
    scale = jnp.full((total_orders, 1), 1.0 / lon_count, jnp.float32)
    cosine, sine = zonal_tables(crossed_orders, longitudes, lon_count, scale, -scale)
    spectral_grad = jnp.einsum(
        "mkc,mn->knc", by_lat[:, 0], cosine, preferred_element_type=jnp.float32
    )
    spectral_grad = spectral_grad + jnp.einsum(
        "mkc,mn->knc", by_lat[:, 1], sine, preferred_element_type=jnp.float32
    )
    grid_grad = (out_grad + spectral_grad).astype(jnp.bfloat16)
    return (grid_grad, gain_grad)


CHUNK = 16
F32 = jnp.float32
BF16 = jnp.bfloat16
MESH = pl.DeviceIdType.MESH


def base_tables(order_count, lon_count):
    phase = np.arange(order_count)[:, None] * np.arange(lon_count)[None, :] % lon_count
    angle = phase.astype(np.float32) * np.float32(2.0 * math.pi / lon_count)
    return np.concatenate([np.cos(angle), -np.sin(angle)], axis=1).astype(jnp.bfloat16)


def dot(a, b):
    return jnp.dot(a, b, preferred_element_type=F32)


def block_kernel(
    lat_size,
    obs_size,
    value_ref,
    lat_frac_ref,
    lon_frac_ref,
    corner_ref,
    channel_ref,
    count_ref,
    order_row,
    quad_row,
    next_hbm,
    act_hbm,
    leg_hbm,
    gain_hbm,
    saved_hbm,
    table_hbm,
    table_t_hbm,
    grid_out,
    gain_out,
    next_ref,
    act_ref,
    leg_ref,
    gain_ref,
    saved_ref,
    table_ref,
    table_t_ref,
    packed,
    obs_in,
    hot,
    hot_t,
    waves,
    tab_t,
    leg_t,
    to_slot,
    to_lat,
    slope_ref,
    out_ref,
    pre_ref,
    fwd_out,
    fwd_in,
    by_slot,
    coeff_ref,
    by_lat,
    bwd_out,
    bwd_in,
    grid_ref,
    total,
    near_out,
    near_in,
    far_out,
    far_in,
    parts,
    local_sem,
    obs_send,
    obs_recv,
    fwd_send,
    fwd_recv,
    bwd_send,
    bwd_recv,
    sum_send,
    sum_recv,
    leave_sem,
):
    group = lat_size * obs_size
    my_lat = lax.axis_index("lat")
    my_obs = lax.axis_index("obs")
    me = my_lat * obs_size + my_obs
    lat_dev, lon_count, width = next_ref.shape
    slot_dev, lat_count, degrees = leg_ref.shape
    orders = order_row.shape[1]
    capacity = value_ref.shape[1]
    chunks = slot_dev // CHUNK
    rows = CHUNK * lat_dev
    lanes = packed.shape[2]
    tile = 256

    others = []
    for j in range(1, group):
        lat_at = lax.rem(my_lat + j % lat_size, lat_size)
        obs_at = lax.rem(my_obs + j // lat_size, obs_size)
        others.append((lat_at * obs_size + obs_at, {"lat": lat_at, "obs": obs_at}))

    def peers(body):
        for peer, where in others:
            body(peer, where)

    def send(src, dst, send_sem, recv_sem, target):
        return pltpu.make_async_remote_copy(
            src_ref=src,
            dst_ref=dst,
            send_sem=send_sem,
            recv_sem=recv_sem,
            device_id=target,
            device_id_type=MESH,
        )

    beside = {"obs": lax.rem(my_obs + 1, obs_size)}

    def iota(shape, axis):
        return lax.broadcasted_iota(jnp.int32, shape, axis)

    def column(row):
        side = row.shape[1]
        same = iota((side, side), 0) == iota((side, side), 1)
        return jnp.sum(jnp.where(same, row, 0.0), axis=1, keepdims=True)

    barrier = pltpu.get_barrier_semaphore()
    peers(
        lambda _, where: pl.semaphore_signal(
            barrier, inc=1, device_id=where, device_id_type=MESH
        )
    )
    local = [
        pltpu.make_async_copy(src, dst, local_sem.at[i])
        for i, (src, dst) in enumerate(
            (
                (act_hbm, act_ref),
                (table_hbm, table_ref),
                (next_hbm, next_ref),
                (table_t_hbm, table_t_ref),
                (leg_hbm, leg_ref),
                (gain_hbm, gain_ref),
                (saved_hbm, saved_ref),
            )
        )
    ]
    for copy in local[:3]:
        copy.start()

    alive = iota((capacity, group), 0) < count_ref[...]
    lat_step = lat_frac_ref[0].astype(F32)
    lon_step = lon_frac_ref[0].astype(F32)
    corner = corner_ref[0]
    fields = (
        jnp.where(alive, value_ref[0].astype(F32), 0.0),
        (1.0 - lat_step) * (1.0 - lon_step),
        (1.0 - lat_step) * lon_step,
        lat_step * (1.0 - lon_step),
        lat_step * lon_step,
        (corner // 128).astype(F32),
        (corner % 128).astype(F32),
        channel_ref[0].astype(F32),
    )
    at_row = iota((8 * group, group), 0)
    at_tile = iota((8 * group, group), 1)
    by_row = jnp.zeros((8 * group, capacity), F32)
    for i, field in enumerate(fields):
        pick = jnp.where(at_row == at_tile * 8 + i, 1.0, 0.0).astype(BF16)
        by_row = by_row + lax.dot_general(
            pick, field.astype(BF16), (((1,), (1,)), ((), ())), preferred_element_type=F32
        )
    spots = lanes // capacity
    spread = jnp.where(
        iota((capacity, lanes), 1) == lax.rem(me, spots) * capacity + iota((capacity, lanes), 0),
        1.0,
        0.0,
    ).astype(BF16)
    packed[...] = dot(by_row.astype(BF16), spread).reshape(group, 8, lanes)
    obs_in[me] = packed[me]

    order_f = order_row[...].astype(F32)
    order_col = column(order_f).reshape(group, chunks, CHUNK, 1)
    per = orders // chunks
    for q in range(chunks):
        here = order_col[:, q].reshape(per, 1)
        hot[q] = jnp.where(iota((per, orders), 1).astype(F32) == here, 1.0, 0.0).astype(BF16)

    pl.semaphore_wait(barrier, group - 1)
    peers(
        lambda peer, where: send(
            packed.at[peer], obs_in.at[me], obs_send, obs_recv, where
        ).start()
    )
    for copy in local[3:]:
        copy.start()

    local[0].wait()
    for k in range(lat_dev):
        values = act_ref[k].astype(F32)
        cdf = 0.5 * (1.0 + lax.erf(values * 0.7071067811865476))
        density = jnp.exp(-0.5 * values * values) * 0.3989422804014327
        slope_ref[k] = cdf + values * density
    local[2].wait()
    send(
        packed.at[pl.ds(0, group - 1)],
        obs_in.at[pl.ds(0, group - 1)],
        obs_send,
        obs_recv,
        beside,
    ).wait_recv()
    halves = []
    for h in range(group // spots):
        halves.append(jnp.sum(obs_in[h * spots : (h + 1) * spots], axis=0))
    seen = jnp.concatenate(halves, axis=1)
    received = seen.shape[1]
    corner = seen[5:6].astype(jnp.int32) * 128 + seen[6:7].astype(jnp.int32)
    channel = seen[7:8].astype(jnp.int32)
    left = corner % lon_count
    right = corner - left + (left + 1) % lon_count
    places = (corner, right, corner + lon_count, right + lon_count)
    chan_ids = lax.axis_index("chan") * width + iota((width, received), 0)
    amounts = jnp.where(chan_ids == channel, seen[0:1], 0.0).astype(BF16)
    for k in range(lat_dev):
        for half in range(2):
            span = lon_count // 2
            begin = half * span
            cells = k * lon_count + begin + iota((span, received), 0)
            stencil = jnp.zeros((span, received), F32)
            for w, at in enumerate(places):
                stencil = jnp.where(cells == at, seen[1 + w : 2 + w], stencil)
            added = lax.dot_general(
                stencil.astype(BF16), amounts, (((1,), (1,)), ((), ())), preferred_element_type=F32
            )
            here = slice(begin, begin + span)
            out_grad = next_ref[k, here].astype(F32) + added
            out_ref[k, here] = out_grad
            pre_ref[here, k * width : (k + 1) * width] = (out_grad * slope_ref[k, here]).astype(BF16)

    local[1].wait()
    factor = jnp.where(iota((orders, 1), 0) == 0, 1.0, 2.0)
    for part in range(2):
        got = dot(table_ref[:, part * lon_count : (part + 1) * lon_count], pre_ref[...])
        for k in range(lat_dev):
            begin = (k * 2 + part) * width
            waves[:, begin : begin + width] = (
                got[:, k * width : (k + 1) * width] * factor
            ).astype(BF16)

    def zonal(q, carry):
        got = dot(hot[q], waves[...]).reshape(group, CHUNK, lat_dev * 2 * width)
        fwd_out[q] = jnp.concatenate(
            [got[:, :, k * 2 * width : (k + 1) * 2 * width] for k in range(lat_dev)], axis=1
        ).astype(BF16)
        fwd_in[q, me] = fwd_out[q, me]
        peers(
            lambda peer, where: send(
                fwd_out.at[q, peer], fwd_in.at[q, me], fwd_send, fwd_recv.at[q], where
            ).start()
        )
        return carry

    lax.fori_loop(0, chunks, zonal, 0)

    side = lat_count * CHUNK
    first = iota((side, side), 0)
    second = iota((side, side), 1)
    to_lat[...] = jnp.where(
        (first // CHUNK == second % lat_count) & (first % CHUNK == second // lat_count), 1.0, 0.0
    ).astype(BF16)
    to_slot[...] = jnp.where(
        (second // CHUNK == first % lat_count) & (second % CHUNK == first // lat_count), 1.0, 0.0
    ).astype(BF16)
    joined = lanes // lat_count
    for copy in local[4:]:
        copy.wait()

    def turn(j, carry):
        table = leg_ref[pl.ds(j * joined, joined)].reshape(lanes, degrees)
        leg_t[j] = table.T
        return carry

    lax.fori_loop(0, slot_dev // joined, turn, 0)
    total[...] = jnp.zeros_like(total)
    quad = column(quad_row[...])

    def make_tab_t(part):
        def step(i, carry):
            at = pl.multiple_of(i * tile, tile)
            got = dot(table_t_ref[pl.ds(part * lon_count + at, tile), :], hot_t[...])
            tab_t[pl.ds(at, tile), part * orders : (part + 1) * orders] = got.astype(BF16)
            return carry

        lax.fori_loop(0, lon_count // tile, step, 0)

    share = degrees // group

    def around(axis, size, mine, src, dst, sem):
        def step(j, carry):
            peer = lax.rem(mine + j, size)
            send(
                src.at[peer],
                dst.at[mine],
                sum_send.at[sem],
                sum_recv.at[sem],
                {axis: peer},
            ).start()
            return carry

        lax.fori_loop(1, size, step, 0)

    def landed(axis, size, mine, src, dst, sem):
        return send(
            src.at[pl.ds(0, size - 1)],
            dst.at[pl.ds(0, size - 1)],
            sum_send.at[sem],
            sum_recv.at[sem],
            {axis: lax.rem(mine + 1, size)},
        )

    stages = (
        ("obs", obs_size, my_obs, near_out, near_in, 0),
        ("lat", lat_size, my_lat, far_out, far_in, 1),
        ("lat", lat_size, my_lat, far_out, far_in, 2),
        ("obs", obs_size, my_obs, parts, parts, 3),
    )
    def start_sum():
        for r in range(2):
            near_out[:, :, r * share : (r + 1) * share, :] = (
                total[r].reshape(obs_size, lat_size, share, width).astype(BF16)
            )
        near_in[my_obs] = near_out[my_obs]
        around(*stages[0])

    span = 128

    def degrees_of(q, carry):
        send(
            fwd_out.at[q, pl.ds(0, group - 1)],
            fwd_in.at[q, pl.ds(0, group - 1)],
            fwd_send,
            fwd_recv.at[q],
            beside,
        ).wait_recv()
        arrived = dot(to_slot[...], fwd_in[q].reshape(side, 2 * width)).astype(BF16)
        owner = iota((lanes, 2 * width), 0) // lat_count
        for i in range(CHUNK):
            begin = i // joined * lanes
            by_slot[i] = jnp.where(
                owner == i % joined, arrived[begin : begin + lanes].astype(F32), 0.0
            ).astype(BF16)

        def degree_tile(t, inner):
            here = pl.ds(pl.multiple_of(t * span, span), span)
            gain_real = gain_ref[0, here, :]
            gain_imag = gain_ref[1, here, :]
            sum_real = total[0, here, :]
            sum_imag = total[1, here, :]
            for i in range(CHUNK):
                s = q * CHUNK + i
                up = dot(leg_t[q * (CHUNK // joined) + i // joined, here, :], by_slot[i])
                up_real = up[:, :width]
                up_imag = up[:, width:]
                saved_real = saved_ref[s, 0, here, :].astype(F32)
                saved_imag = saved_ref[s, 1, here, :].astype(F32)
                sum_real = sum_real + (up_real * saved_real + up_imag * saved_imag)
                sum_imag = sum_imag + (up_imag * saved_real - up_real * saved_imag)
                coeff_ref[i, here, :width] = (
                    gain_real * up_real + gain_imag * up_imag
                ).astype(BF16)
                coeff_ref[i, here, width:] = (
                    gain_real * up_imag - gain_imag * up_real
                ).astype(BF16)
            total[0, here, :] = sum_real
            total[1, here, :] = sum_imag
            return inner

        lax.fori_loop(0, degrees // span, degree_tile, 0)
        pl.when(q == chunks - 1)(start_sum)
        for i in range(CHUNK):
            by_lat[i * lat_count : (i + 1) * lat_count, :] = (
                dot(leg_ref[q * CHUNK + i], coeff_ref[i]) * quad
            ).astype(BF16)
        bwd_out[q] = dot(to_lat[...], by_lat[...]).astype(BF16).reshape(group, rows, 2 * width)
        bwd_in[me, q] = bwd_out[q, me]
        peers(
            lambda peer, where: send(
                bwd_out.at[q, peer], bwd_in.at[me, q], bwd_send, bwd_recv, where
            ).start()
        )
        return carry

    lax.fori_loop(0, chunks, degrees_of, 0)

    hot_t[...] = jnp.where(iota((orders, orders), 0) == order_row[...], 1.0, 0.0).astype(BF16)
    local[3].wait()
    make_tab_t(0)
    landed(*stages[0]).wait_recv()
    far_out[...] = jnp.sum(near_in[...].astype(F32), axis=0).astype(BF16)
    far_in[my_lat] = far_out[my_lat]
    around(*stages[1])
    make_tab_t(1)
    landed(*stages[1]).wait_recv()
    parts[my_obs, my_lat] = jnp.sum(far_in[...].astype(F32), axis=0).astype(BF16)

    def spread_out(j, carry):
        peer = lax.rem(my_lat + j, lat_size)
        send(
            parts.at[my_obs, my_lat],
            parts.at[my_obs, my_lat],
            sum_send.at[2],
            sum_recv.at[2],
            {"lat": peer},
        ).start()
        return carry

    lax.fori_loop(1, lat_size, spread_out, 0)

    landed(*stages[2]).wait_recv()

    def spread_wide(j, carry):
        send(
            parts.at[my_obs],
            parts.at[my_obs],
            sum_send.at[3],
            sum_recv.at[3],
            {"obs": lax.rem(my_obs + j, obs_size)},
        ).start()
        return carry

    lax.fori_loop(1, obs_size, spread_wide, 0)

    send(
        bwd_out.at[:, pl.ds(0, group - 1)],
        bwd_in.at[pl.ds(0, group - 1)],
        bwd_send,
        bwd_recv,
        beside,
    ).wait_recv()

    back = bwd_in[...].astype(F32).reshape(group * chunks, lat_dev, CHUNK, 2 * width)
    for part in range(2):
        lane = slice(part * width, (part + 1) * width)
        pre_ref[part * orders : (part + 1) * orders, :] = jnp.concatenate(
            [back[:, k, :, lane].reshape(orders, width) for k in range(lat_dev)], axis=1
        ).astype(BF16)

    leaving = []
    for i in range(lon_count // tile):
        here = slice(i * tile, (i + 1) * tile)
        got = dot(tab_t[here, :], pre_ref[0 : 2 * orders, :]) * (1.0 / lon_count)
        for k in range(lat_dev):
            grid_ref[k, here, :] = (
                out_ref[k, here, :] + got[:, k * width : (k + 1) * width]
            ).astype(BF16)
        leaving.append(
            pltpu.make_async_copy(grid_ref.at[:, here], grid_out.at[:, here], leave_sem.at[i])
        )
        leaving[-1].start()

    landed(*stages[3]).wait_recv()
    for r in range(2):
        leaving.append(
            pltpu.make_async_copy(
                parts.at[:, :, r * share : (r + 1) * share],
                gain_out.at[r],
                leave_sem.at[lon_count // tile + r],
            )
        )
        leaving[-1].start()

    send(
        packed.at[pl.ds(0, group - 1)], obs_in.at[pl.ds(0, group - 1)], obs_send, obs_recv, beside
    ).wait_send()
    send(
        fwd_out.at[:, pl.ds(0, group - 1)],
        fwd_in.at[:, pl.ds(0, group - 1)],
        fwd_send,
        fwd_recv.at[0],
        beside,
    ).wait_send()
    send(
        bwd_out.at[:, pl.ds(0, group - 1)],
        bwd_in.at[pl.ds(0, group - 1)],
        bwd_send,
        bwd_recv,
        beside,
    ).wait_send()
    landed(*stages[0]).wait_send()
    landed(*stages[1]).wait_send()
    landed(*stages[2]).wait_send()
    landed(*stages[3]).wait_send()
    for copy in leaving:
        copy.wait()


def on_device(
    next_grad,
    pre_act,
    legendre,
    order_slots,
    quad_weights,
    spectral_gain,
    saved_coeffs,
    obs_value,
    obs_lat_frac,
    obs_lon_frac,
    obs_corner,
    obs_channel,
    slot_counts,
):
    lat_dev, lon_count, width = next_grad.shape
    lat_size = lax.axis_size("lat")
    obs_size = lax.axis_size("obs")
    group = lat_size * obs_size
    slot_dev, degrees, lat_count = legendre.shape
    orders = order_slots.shape[0]
    chunks = slot_dev // CHUNK
    rows = CHUNK * lat_dev
    lanes = 128
    side = lat_count * CHUNK
    joined = lanes // lat_count
    table = base_tables(orders, lon_count)
    table_t = np.ascontiguousarray(table.T)

    vmem = pl.BlockSpec(memory_space=pltpu.VMEM)
    anywhere = pl.BlockSpec(memory_space=pltpu.HBM)
    dma = pltpu.SemaphoreType.DMA
    share = degrees // group
    grid_grad, gain_parts = pl.pallas_call(
        functools.partial(block_kernel, lat_size, obs_size),
        out_shape=(
            jax.ShapeDtypeStruct((lat_dev, lon_count, width), BF16),
            jax.ShapeDtypeStruct((2, obs_size, lat_size, share, width), BF16),
        ),
        in_specs=[vmem] * 8 + [anywhere] * 7,
        out_specs=(pl.BlockSpec(memory_space=pl.ANY), pl.BlockSpec(memory_space=pl.ANY)),
        scratch_shapes=[
            pltpu.VMEM((lat_dev, lon_count, width), BF16),
            pltpu.VMEM((lat_dev, lon_count, width), BF16),
            pltpu.VMEM((slot_dev, lat_count, degrees), BF16),
            pltpu.VMEM((2, degrees, width), F32),
            pltpu.VMEM((slot_dev, 2, degrees, width), BF16),
            pltpu.VMEM((orders, 2 * lon_count), BF16),
            pltpu.VMEM((2 * lon_count, orders), BF16),
            pltpu.VMEM((group, 8, lanes), F32),
            pltpu.VMEM((group, 8, lanes), F32),
            pltpu.VMEM((chunks, orders // chunks, orders), BF16),
            pltpu.VMEM((orders, orders), BF16),
            pltpu.VMEM((orders, lat_dev * 2 * width), BF16),
            pltpu.VMEM((lon_count, 2 * orders), BF16),
            pltpu.VMEM((slot_dev // joined, degrees, lanes), BF16),
            pltpu.VMEM((side, side), BF16),
            pltpu.VMEM((side, side), BF16),
            pltpu.VMEM((lat_dev, lon_count, width), F32),
            pltpu.VMEM((lat_dev, lon_count, width), F32),
            pltpu.VMEM((max(lon_count, 2 * orders), lat_dev * width), BF16),
            pltpu.VMEM((chunks, group, rows, 2 * width), BF16),
            pltpu.VMEM((chunks, group, rows, 2 * width), BF16),
            pltpu.VMEM((CHUNK, lanes, 2 * width), BF16),
            pltpu.VMEM((CHUNK, degrees, 2 * width), BF16),
            pltpu.VMEM((side, 2 * width), BF16),
            pltpu.VMEM((chunks, group, rows, 2 * width), BF16),
            pltpu.VMEM((group, chunks, rows, 2 * width), BF16),
            pltpu.VMEM((lat_dev, lon_count, width), BF16),
            pltpu.VMEM((2, degrees, width), F32),
            pltpu.VMEM((obs_size, lat_size, 2 * share, width), BF16),
            pltpu.VMEM((obs_size, lat_size, 2 * share, width), BF16),
            pltpu.VMEM((lat_size, 2 * share, width), BF16),
            pltpu.VMEM((lat_size, 2 * share, width), BF16),
            pltpu.VMEM((obs_size, lat_size, 2 * share, width), BF16),
            dma((7,)),
            dma,
            dma,
            dma,
            dma((chunks,)),
            dma,
            dma,
            dma((4,)),
            dma((4,)),
            dma((lon_count // 256 + 2,)),
        ],
        compiler_params=pltpu.CompilerParams(
            collective_id=0, has_side_effects=True, vmem_limit_bytes=60 * 1024 * 1024
        ),
        name="block_backward",
    )(
        obs_value,
        obs_lat_frac,
        obs_lon_frac,
        obs_corner,
        obs_channel,
        slot_counts,
        order_slots[None, :],
        quad_weights[None, :],
        next_grad,
        pre_act,
        jnp.transpose(legendre, (0, 2, 1)),
        spectral_gain,
        saved_coeffs,
        jnp.asarray(table),
        jnp.asarray(table_t),
    )
    return grid_grad, gain_parts.astype(F32).reshape(2, degrees, width)


def kernel_fits(next_grad, legendre, obs_value, lat_size, obs_size):
    group = lat_size * obs_size
    lat_dev, lon_count, width = next_grad.shape
    slot_dev, degrees, lat_count = legendre.shape
    capacity = obs_value.shape[1]
    return (
        slot_dev % CHUNK == 0
        and (CHUNK * lat_dev) % 16 == 0
        and lat_count * CHUNK <= 512
        and 128 % lat_count == 0
        and CHUNK % (128 // lat_count) == 0
        and degrees % 128 == 0
        and lat_size > 1
        and obs_size > 1
        and width % 128 == 0
        and lon_count % 512 == 0
        and degrees % (16 * group) == 0
        and 128 % capacity == 0
        and group % (128 // capacity) == 0
    )


def device_path(*args):
    if kernel_fits(args[0], args[2], args[7], lax.axis_size("lat"), lax.axis_size("obs")):
        return on_device(*args)
    return plain_path(*args)


def solution(mesh):
    in_specs = (
        P(("lat", "obs"), None, "chan"),
        P(("lat", "obs"), None, "chan"),
        P(("lat", "obs"), None, None),
        P(),
        P(),
        P(None, None, "chan"),
        P(("lat", "obs"), None, None, "chan"),
        P(("lat", "obs"), None, None),
        P(("lat", "obs"), None, None),
        P(("lat", "obs"), None, None),
        P(("lat", "obs"), None, None),
        P(("lat", "obs"), None, None),
        P(("lat", "obs"), None),
    )
    out_specs = (P(("lat", "obs"), None, "chan"), P(None, None, "chan"))
    return jax.shard_map(
        device_path, mesh=mesh, in_specs=in_specs, out_specs=out_specs, check_vma=False
    )
```
